512 devices in a mesh: fsdp: 64 (over x, y, core), replica: 8 (over z).
Axes of the slice: x: 4, y: 8, z: 8, core: 2. Of those that a mesh axis runs over, the one named last changes fastest.
Arguments:
- gradient: bfloat16 [16, 1024, 8, 1024], P(None, 'fsdp', None, 'replica')
- second_moment: bfloat16 [16, 1024, 8, 1024], P(None, 'fsdp', None, 'replica'), may hold values from 0.25 to 4
- momentum: bfloat16 [16, 1024, 8, 1024], P(None, 'fsdp', None, 'replica'), may hold values from -3 to 3
- left_factor: bfloat16 [192, 1024, 1024], P('fsdp', 'replica')
- right_factor: bfloat16 [192, 1024, 1024], P('fsdp', None, 'replica')
- block_of_slot: int32 [64, 3], replicated, may hold values from -1 to 127, as said below
Outputs:
- momentum_new: bfloat16 [16, 1024, 8, 1024], P(None, 'fsdp', None, 'replica')
- moment_new: bfloat16 [16, 1024, 8, 1024], P(None, 'fsdp', None, 'replica')
The draws below stay inside these ranges and needn't reach their ends.
Inputs may be any that keep to these rules, and one draw needn't show every extreme that they name: `block_of_slot`: every block appears in exactly one slot; an owner holds 0 to 3 blocks and at least one owner holds exactly 3; all other slots hold -1.
All inputs are finite; a program needn't handle non-finite values.
Results may differ from the reference program's by a relative error of at most 0.0057.
Values may be sent and summed in bfloat16 or wider, within the bound.
No kernel may reach another device: no remote copies, remote signals or barrier semaphores. Data moves between devices by JAX's collectives and lax.ppermute only.
A program may use at most 64 MiB of HBM per device.

```python
import math
import jax
import jax.numpy as jnp
from jax import lax

B = 1024
BC = 8
BROWS = 16
NBLK = 128
SLOTS = 3
N_FSDP = 64


def draw_gradient(key, part):
    key = jax.random.fold_in(key, 3)
    row_key, col_key, entry_key = jax.random.split(key, 3)
    shape = (BROWS, B, BC, B)
    row_scale = jnp.exp(jax.random.uniform(row_key, (BROWS, B, 1, 1), jnp.float32, math.log(0.3), math.log(3.0)))
    col_scale = jnp.exp(jax.random.uniform(col_key, (1, 1, BC, B), jnp.float32, math.log(0.3), math.log(3.0)))
    values = jax.random.normal(entry_key, shape, jnp.float32) * row_scale * col_scale
    return values.astype(jnp.bfloat16)


def with_diagonal(entries, spread):
    identity_mask = (jnp.arange(B)[:, None] == jnp.arange(B)[None, :]).astype(jnp.float32)
    return (identity_mask[None] + entries * (spread / math.sqrt(B))).astype(jnp.bfloat16)


def draw_left_factor(key, part):
    key = jax.random.fold_in(key, 5)
    shape = (N_FSDP * SLOTS, B, B)
    entries = jax.random.normal(key, shape, jnp.float32)
    return with_diagonal(entries, 0.5)


def draw_right_factor(key, part):
    key = jax.random.fold_in(key, 7)
    shape = (N_FSDP * SLOTS, B, B)
    entries = jax.random.normal(key, shape, jnp.float32)
    return with_diagonal(entries, 0.5)


def draw_block_of_slot(key, part):
    key = jax.random.fold_in(key, 11)
    owner_key, shuffle_key, block_key = jax.random.split(key, 3)
    slot_total = N_FSDP * SLOTS
    full_owner = jax.random.randint(owner_key, (), 0, N_FSDP)
    shuffle = jax.random.permutation(shuffle_key, slot_total).astype(jnp.int32)
    owner_of = jnp.arange(slot_total, dtype=jnp.int32) // SLOTS
    priority = jnp.where(owner_of == full_owner, shuffle - slot_total, shuffle)
    position = jnp.argsort(jnp.argsort(priority)).astype(jnp.int32)
    blocks = jax.random.permutation(block_key, NBLK).astype(jnp.int32)
    filled = position < NBLK
    chosen = blocks[jnp.minimum(position, NBLK - 1)]
    return jnp.where(filled, chosen, -1).reshape(N_FSDP, SLOTS).astype(jnp.int32)


def shard_levels(rng, dims, cuts, smallest, top_value):
    def one(axis_at, shards_of):
        draws = jax.random.uniform(jax.random.fold_in(jax.random.fold_in(rng, 6), axis_at), (shards_of,), jnp.float32, smallest / len(cuts), top_value / len(cuts))
        return jnp.repeat(jnp.exp(draws), dims[axis_at] // shards_of).reshape((-1,) + (1,) * (len(dims) - axis_at - 1))

    loudness = one(*cuts[0])
    for cut in cuts[1:]:
        loudness = loudness * one(*cut)
    return loudness


def bell_draw(rng, shape, deviation, bound, cuts=(), kind=jnp.bfloat16):
    result = jax.random.normal(rng, shape, jnp.float32) * deviation
    if len(cuts) > 0:
        result = shard_levels(rng, shape, cuts, -0.22, 0.18) * result
    return jnp.clip(result, min=-bound, max=bound).astype(kind)


def setup_inputs(seed: int = 0) -> dict:
    splits = jax.random.split(jax.random.key(seed), 7)
    return {
        "gradient": draw_gradient(jax.random.fold_in(splits[6], 71), 0),
        "second_moment": jnp.clip(jnp.exp(math.log(4.0) - 2.7725887 * jax.random.uniform(splits[1], (BROWS, B, BC, B), jnp.float32) ** shard_levels(splits[1], (BROWS, B, BC, B), ((1, 64), (3, 8)), -0.2, 0.2)), 0.25, 4.0).astype(jnp.bfloat16),
        "momentum": bell_draw(splits[2], (BROWS, B, BC, B), 0.5, 3.0, ((1, 64), (3, 8))),
        "left_factor": draw_left_factor(jax.random.fold_in(splits[6], 71), 0),
        "right_factor": draw_right_factor(jax.random.fold_in(splits[6], 71), 0),
        "block_of_slot": draw_block_of_slot(jax.random.fold_in(splits[6], 71), 0),
    }


BETA_ONE = 0.9
BETA_TWO = 0.999
ADAM_EPS = 1e-08
NORM_EPS = 1e-06

def adam_terms(gradient_f, second_f):
    moment_new = BETA_TWO * second_f + (1.0 - BETA_TWO) * gradient_f * gradient_f
    return (moment_new, gradient_f / (jnp.sqrt(moment_new) + ADAM_EPS))

def to_blocks(array):
    return jnp.transpose(array, (0, 2, 1, 3)).reshape(NBLK, B, B)

def reference(gradient, second_moment, momentum, left_factor, right_factor, block_of_slot):
    gradient_f = gradient.astype(jnp.float32)
    moment_new, adam_step = adam_terms(gradient_f, second_moment.astype(jnp.float32))
    adam_square = lax.optimization_barrier(jnp.sum(to_blocks(adam_step * adam_step), axis=(1, 2)))
    grad_blocks = to_blocks(gradient)
    slot_block = block_of_slot.reshape(-1)
    slot_live = slot_block >= 0
    target = jnp.where(slot_live, slot_block, NBLK)
    block_place = jnp.zeros((NBLK,), jnp.int32).at[target].set(jnp.arange(N_FSDP * SLOTS, dtype=jnp.int32), mode='drop')

    def precondition(block_index):
        slot_place = block_place[block_index]
        left_rows = left_factor[slot_place]
        right_cols = right_factor[slot_place]
        product = jnp.dot(left_rows, grad_blocks[block_index], preferred_element_type=jnp.float32).astype(jnp.bfloat16)
        shampoo = jnp.dot(product, right_cols, preferred_element_type=jnp.float32)
        graft_scale = jnp.sqrt(adam_square[block_index]) / jnp.sqrt(jnp.sum(shampoo * shampoo) + NORM_EPS)
        return (shampoo * graft_scale).astype(jnp.bfloat16)
    grafted = lax.map(precondition, jnp.arange(NBLK, dtype=jnp.int32))
    grafted = jnp.transpose(grafted.reshape(BROWS, BC, B, B), (0, 2, 1, 3))
    momentum_new = BETA_ONE * momentum.astype(jnp.float32) + grafted.astype(jnp.float32)
    return (momentum_new.astype(jnp.bfloat16), moment_new.astype(jnp.bfloat16))
```

```python
import jax
import jax.numpy as jnp
from jax import lax
from jax.experimental import pallas as pl
from jax.experimental.pallas import tpu as pltpu
from jax.sharding import Mesh
from jax.sharding import PartitionSpec as P

BETA_ONE = 0.9
BETA_TWO = 0.999
ADAM_EPS = 1e-08
NORM_EPS = 1e-06

COL = ("x1", "x0", "y2", "y1", "y0")
REPLICA = ("z2", "z1", "z0")
RING = 8
COLS = 32
SLOTS = 3
PLACES = 4
CORES = 2
NOTE = 3

ANY = pl.BlockSpec(memory_space=pl.ANY)
VMEM = pl.BlockSpec(memory_space=pltpu.VMEM)
SMEM = pl.BlockSpec(memory_space=pltpu.SMEM)


def limit(mebibytes):
    return pltpu.CompilerParams(vmem_limit_bytes=mebibytes * 1024 * 1024)


def high_low(value):
    high = value.astype(jnp.bfloat16).astype(jnp.float32)
    return high, value - high


def member(col, place):
    return col * RING + place


def factor_pairs(step):
    pairs = []
    for c in range(CORES):
        for s in range(SLOTS):
            root = PLACES * c + s
            near, far = (root + step) % RING, (root + step + PLACES) % RING
            if step > 0:
                pairs.append((c * RING + near, c * RING + root))
            pairs.append((c * RING + far, (1 - c) * RING + root))
    return pairs


def factor_kernel(left, right, *outs):
    part = left.shape[1]
    here = lax.axis_index(REPLICA)
    for step in range(PLACES):
        slot = lax.rem(here - step + RING, PLACES)

        @pl.when(slot < SLOTS)
        def _():
            for j in range(RING):
                outs[step][j] = left[slot, :, j * part : (j + 1) * part]
                outs[step][RING + j] = right[slot, j * part : (j + 1) * part, :]


def spread_factors(left, right):
    part = left.shape[1]
    return pl.pallas_call(
        factor_kernel,
        out_shape=[jax.ShapeDtypeStruct((2 * RING, part, part), left.dtype)] * PLACES,
        in_specs=[VMEM, VMEM],
        out_specs=[VMEM] * PLACES,
        compiler_params=limit(16),
        name="spread_factors",
    )(left, right)


def prepare_kernel(slots, gradient, second, after, moment, pieces, place, wide, square, notes):
    block_rows, shard_rows, block_cols, lanes = gradient.shape
    per_row = shard_rows * block_cols

    def adam(i, carry):
        g = gradient[i].astype(jnp.float32)
        v = BETA_TWO * second[i].astype(jnp.float32) + (1.0 - BETA_TWO) * g * g
        moment[i] = v.astype(moment.dtype)
        step = g / (jnp.sqrt(v) + ADAM_EPS)
        square[pl.ds(pl.multiple_of(i * block_cols, block_cols), block_cols), :] = jnp.sum(step * step, axis=0)
        wide[pl.ds(pl.multiple_of(i * per_row, per_row), per_row), :] = g.reshape(per_row, lanes)
        return carry

    lax.fori_loop(0, block_rows, adam, 0)
    notes[...] = jnp.zeros(notes.shape, notes.dtype)

    def column(col, carry):
        for c in range(CORES):
            for s in range(SLOTS):
                held = slots[col * CORES + c, s]
                block = jnp.maximum(held, 0)
                i = lax.div(block, block_cols)
                j = lax.rem(block, block_cols)
                piece = wide[pl.ds(i * per_row + j, shard_rows, stride=block_cols), :]
                pieces[member(col, PLACES * c + s)] = piece.astype(pieces.dtype)
                high, low = high_low(square[pl.ds(block, 1), :])
                row = 2 * (SLOTS * c + s)
                notes[row : row + 1, :] = high
                notes[row + 1 : row + 2, :] = low

                @pl.when(held >= 0)
                def _():
                    place[0, block] = member(col, PLACES * c + s)
                    place[1, block] = col * shard_rows + row

        pieces[member(col, NOTE)] = notes[...].astype(pieces.dtype)
        return carry

    lax.fori_loop(0, COLS, column, 0)


def prepare(slots, gradient, second, after):
    block_rows, shard_rows, block_cols, lanes = gradient.shape
    block_count = block_rows * block_cols
    return pl.pallas_call(
        prepare_kernel,
        out_shape=[
            jax.ShapeDtypeStruct(second.shape, second.dtype),
            jax.ShapeDtypeStruct((COLS * RING, shard_rows, lanes), gradient.dtype),
            jax.ShapeDtypeStruct((2, block_count), jnp.int32),
        ],
        in_specs=[SMEM, VMEM, VMEM, ANY],
        out_specs=[VMEM, VMEM, SMEM],
        scratch_shapes=[
            pltpu.VMEM((block_count * shard_rows, lanes), jnp.float32),
            pltpu.VMEM((block_count, lanes), jnp.float32),
            pltpu.VMEM((shard_rows, lanes), jnp.float32),
        ],
        compiler_params=limit(16),
        name="prepare",
    )(slots, gradient, second, after)


def together_kernel(columns, own, *refs):
    factors, out = refs[:PLACES], refs[PLACES]
    count = columns.shape[0]
    size = own.shape[0] * own.shape[1] // columns.shape[1]
    at_home = lax.div(lax.axis_index(REPLICA), PLACES) == lax.axis_index("core")
    out[:count] = columns[...]
    for step in range(1, PLACES):
        out[count + step * size : count + (step + 1) * size] = factors[step][...].reshape((size,) + columns.shape[1:])

    @pl.when(at_home)
    def _():
        out[count : count + size] = own[...].reshape((size,) + columns.shape[1:])

    @pl.when(jnp.logical_not(at_home))
    def _():
        out[count : count + size] = factors[0][...].reshape((size,) + columns.shape[1:])


def together(columns, own, factors):
    count, rows, part = columns.shape
    count += PLACES * own.shape[0] * own.shape[1] // rows
    return pl.pallas_call(
        together_kernel,
        out_shape=jax.ShapeDtypeStruct((count, rows, part), columns.dtype),
        in_specs=[VMEM] * (2 + PLACES),
        out_specs=VMEM,
        compiler_params=limit(16),
        name="together",
    )(columns, own, *factors)


def block_kernel(own, swapped, out, lf, rf, grad, half, full, notes):
    rows, part = own.shape[1:]
    order = lf.shape[0]
    count = COLS * RING
    groups = part // rows
    core = lax.axis_index("core")
    here = lax.axis_index(REPLICA)
    place = lax.rem(here, PLACES)

    @pl.when(place < SLOTS)
    def _():
        owner_core = lax.div(here, PLACES)
        for b, held in enumerate((own, swapped)):
            h = core if b == 0 else 1 - core
            for col in range(COLS):
                for r in range(RING):
                    grad[col, h, :, r * part : (r + 1) * part] = held[member(col, r)]
            for step in range(PLACES):
                source = lax.rem(here + step + jnp.where(h == owner_core, 0, PLACES), RING)
                at = pl.ds(pl.multiple_of(source * part, part), part)
                for j in range(RING):
                    left = count + (2 * RING * step + j) * groups
                    right = left + RING * groups
                    lf[at, j * part : (j + 1) * part] = held[left : left + groups].reshape(part, part)
                    rf[j * part : (j + 1) * part, at] = held[right : right + groups].reshape(part, part)

        tile = 2 * part
        steps = order // tile

        def first(t, carry):
            at = pl.ds(pl.multiple_of(t * tile, tile), tile)
            rhs = grad[:, :, :, at].reshape(order, tile)
            half[:, at] = jnp.dot(lf[...], rhs, preferred_element_type=jnp.float32).astype(half.dtype)
            return carry

        lax.fori_loop(0, steps, first, 0, unroll=True)

        def second(t, square):
            at = pl.ds(pl.multiple_of(t * tile, tile), tile)
            value = jnp.dot(half[...], rf[:, at], preferred_element_type=jnp.float32)
            full[:, :, :, at] = value.reshape(COLS, CORES, rows, tile)
            return square + jnp.sum(value * value, axis=0, keepdims=True)

        square = lax.fori_loop(0, steps, second, jnp.zeros((1, tile), jnp.float32), unroll=True)
        square = jnp.sum(square, axis=1, keepdims=True)
        scale = 1.0 / jnp.sqrt(square + NORM_EPS)
        for r in range(RING):
            value = (full[:, core, :, r * part : (r + 1) * part] * scale).astype(out.dtype)
            for col in range(COLS):
                out[member(col, r)] = value[col]

    @pl.when(place == NOTE)
    def _():
        total = jnp.zeros(notes.shape, jnp.float32)
        for held in (own, swapped):
            total = total + jnp.sum(held[:count].astype(jnp.float32), axis=0)
        notes[...] = total
        for row in range(0, 2 * CORES * SLOTS, 2):
            high, low = high_low(notes[row : row + 1, :] + notes[row + 1 : row + 2, :])
            notes[row : row + 1, :] = high
            notes[row + 1 : row + 2, :] = low
        out[...] = jnp.broadcast_to(notes[...].astype(out.dtype), out.shape)


def precondition(own, swapped):
    _, rows, part = own.shape
    order = RING * part
    kind = own.dtype
    return pl.pallas_call(
        block_kernel,
        out_shape=jax.ShapeDtypeStruct((COLS * RING, rows, part), kind),
        in_specs=[VMEM] * 2,
        out_specs=VMEM,
        scratch_shapes=[
            pltpu.VMEM((order, order), kind),
            pltpu.VMEM((order, order), kind),
            pltpu.VMEM((COLS, CORES, rows, order), kind),
            pltpu.VMEM((order, order), kind),
            pltpu.VMEM((COLS, CORES, rows, order), jnp.float32),
            pltpu.VMEM((rows, part), jnp.float32),
        ],
        compiler_params=limit(28),
        cost_estimate=pl.CostEstimate(flops=4 * order**3, bytes_accessed=10 * order * order, transcendentals=0),
        name="precondition",
    )(own, swapped)


def finish_kernel(place, returned, momentum, out, wide, adam):
    block_rows, shard_rows, block_cols, lanes = momentum.shape
    for col in range(COLS):
        note = jnp.sum(returned[member(col, NOTE)].astype(jnp.float32), axis=1, keepdims=True)
        adam[col * shard_rows : (col + 1) * shard_rows, :] = jnp.broadcast_to(note, (shard_rows, lanes))

    def step(i, carry):
        for j in range(block_cols):
            block = i * block_cols + j
            row = place[1, block]
            scale = jnp.sqrt(adam[pl.ds(row, 1), :] + adam[pl.ds(row + 1, 1), :])
            piece = returned[place[0, block]].astype(jnp.float32) * scale
            wide[pl.ds(j, shard_rows, stride=block_cols), :] = piece
        grafted = wide[...].reshape(shard_rows, block_cols, lanes)
        out[i] = (BETA_ONE * momentum[i].astype(jnp.float32) + grafted).astype(out.dtype)
        return carry

    lax.fori_loop(0, block_rows, step, 0)


def finish(place, returned, momentum):
    block_rows, shard_rows, block_cols, lanes = momentum.shape
    return pl.pallas_call(
        finish_kernel,
        out_shape=jax.ShapeDtypeStruct(momentum.shape, momentum.dtype),
        in_specs=[SMEM, VMEM, VMEM],
        out_specs=VMEM,
        scratch_shapes=[
            pltpu.VMEM((shard_rows * block_cols, lanes), jnp.float32),
            pltpu.VMEM((COLS * shard_rows, lanes), jnp.float32),
        ],
        compiler_params=limit(16),
        name="finish",
    )(place, returned, momentum)


def exchange(array):
    return lax.all_to_all(array, COL + REPLICA, split_axis=0, concat_axis=0, tiled=True)


def swap(array):
    return lax.ppermute(array, "core", [(0, 1), (1, 0)])


def local(gradient, second_moment, momentum, left_factor, right_factor, block_of_slot):
    spread = spread_factors(left_factor, right_factor)
    factors = [
        lax.ppermute(shard, ("core",) + REPLICA, factor_pairs(step)) for step, shard in enumerate(spread)
    ]
    moment_new, pieces, place = prepare(block_of_slot, gradient, second_moment, spread[0])
    any_live = jnp.any(block_of_slot >= 0)
    columns = lax.cond(any_live, exchange, jnp.zeros_like, pieces)
    held = together(columns, spread[0], factors)
    parts = precondition(held, swap(held))
    return (finish(place, exchange(parts), momentum), moment_new)


def solution(mesh):
    fine = Mesh(mesh.devices.reshape((2,) * 9), COL + ("core",) + REPLICA)
    fsdp = COL + ("core",)
    in_specs = (
        P(None, fsdp, None, REPLICA),
        P(None, fsdp, None, REPLICA),
        P(None, fsdp, None, REPLICA),
        P(fsdp, REPLICA, None),
        P(fsdp, None, REPLICA),
        P(),
    )
    out_specs = (P(None, fsdp, None, REPLICA), P(None, fsdp, None, REPLICA))
    return jax.shard_map(local, mesh=fine, in_specs=in_specs, out_specs=out_specs, check_vma=False)
```

```python
import jax
import jax.numpy as jnp
from jax import lax
from jax.experimental import pallas as pl
from jax.experimental.pallas import tpu as pltpu
from jax.sharding import Mesh
from jax.sharding import PartitionSpec as P

BETA_ONE = 0.9
BETA_TWO = 0.999
ADAM_EPS = 1e-08
NORM_EPS = 1e-06

COL = ("x", "y")
SHAPE = (4, 8, 2, 8)
RING = 8
COLS = 32
SLOTS = 3
PLACES = 4
CORES = 2
NOTE = 3
CHUNKS = 4

ANY = pl.BlockSpec(memory_space=pl.ANY)
HBM = pl.BlockSpec(memory_space=pltpu.HBM)
VMEM = pl.BlockSpec(memory_space=pltpu.VMEM)
SMEM = pl.BlockSpec(memory_space=pltpu.SMEM)


def limit(mebibytes):
    return pltpu.CompilerParams(vmem_limit_bytes=mebibytes * 1024 * 1024)


def high_low(value):
    high = value.astype(jnp.bfloat16).astype(jnp.float32)
    return high, value - high


def member(col, place):
    return col * RING + place


def factor_pairs(step):
    pairs = []
    for c in range(CORES):
        for s in range(SLOTS):
            root = PLACES * c + s
            near, far = (root + step) % RING, (root + step + PLACES) % RING
            if step > 0:
                pairs.append((c * RING + near, c * RING + root))
            pairs.append((c * RING + far, (1 - c) * RING + root))
    return pairs


def factor_kernel(left, right, *refs):
    outs, held_left, held_right, sems = refs[:PLACES], *refs[PLACES:]
    part = left.shape[1]
    here = lax.axis_index("replica")
    copies = []
    for s in range(SLOTS):
        copies.append(pltpu.make_async_copy(left.at[s], held_left.at[s], sems.at[0, s]))
        copies.append(pltpu.make_async_copy(right.at[s], held_right.at[s], sems.at[1, s]))
    for copy in copies:
        copy.start()
    for copy in copies:
        copy.wait()
    for step in range(PLACES):
        slot = lax.rem(here - step + RING, PLACES)

        @pl.when(slot < SLOTS)
        def _():
            for j in range(RING):
                outs[step][j] = held_left[slot, :, j * part : (j + 1) * part]
                outs[step][RING + j] = held_right[slot, j * part : (j + 1) * part, :]


def spread_factors(left, right):
    part = left.shape[1]
    return pl.pallas_call(
        factor_kernel,
        out_shape=[jax.ShapeDtypeStruct((2 * RING, part, part), left.dtype)] * PLACES,
        in_specs=[HBM, HBM],
        out_specs=[VMEM] * PLACES,
        scratch_shapes=[
            pltpu.VMEM(left.shape, left.dtype),
            pltpu.VMEM(right.shape, right.dtype),
            pltpu.SemaphoreType.DMA((2, SLOTS)),
        ],
        compiler_params=limit(63),
        name="spread_factors",
    )(left, right)


def prepare_kernel(slots, gradient, second, after, moment, pieces, place, *scratch):
    held_gradient, held_second, held_moment, wide, square, notes, sems = scratch
    block_rows, shard_rows, block_cols, lanes = gradient.shape
    per_row = shard_rows * block_cols
    chunk = block_rows // CHUNKS
    chunks = [pl.ds(at * chunk, chunk) for at in range(CHUNKS)]
    first, second_in, out = [], [], []
    for at, rows in enumerate(chunks):
        first.append(pltpu.make_async_copy(gradient.at[rows], held_gradient.at[rows], sems.at[0, at]))
        second_in.append(pltpu.make_async_copy(second.at[rows], held_second.at[rows], sems.at[1, at]))
        out.append(pltpu.make_async_copy(held_moment.at[rows], moment.at[rows], sems.at[2, at]))
        first[at].start()
        second_in[at].start()

    def adam(i, carry):
        g = held_gradient[i].astype(jnp.float32)
        v = BETA_TWO * held_second[i].astype(jnp.float32) + (1.0 - BETA_TWO) * g * g
        held_moment[i] = v.astype(moment.dtype)
        step = g / (jnp.sqrt(v) + ADAM_EPS)
        square[pl.ds(pl.multiple_of(i * block_cols, block_cols), block_cols), :] = jnp.sum(step * step, axis=0)
        wide[pl.ds(pl.multiple_of(i * per_row, per_row), per_row), :] = g.reshape(per_row, lanes)
        return carry

    for at in range(CHUNKS):
        first[at].wait()
        second_in[at].wait()
        lax.fori_loop(at * chunk, (at + 1) * chunk, adam, 0)
        out[at].start()
    notes[...] = jnp.zeros(notes.shape, notes.dtype)

    def column(col, carry):
        for c in range(CORES):
            for s in range(SLOTS):
                held = slots[s, col * CORES + c]
                block = jnp.maximum(held, 0)
                i = lax.div(block, block_cols)
                j = lax.rem(block, block_cols)
                piece = wide[pl.ds(i * per_row + j, shard_rows, stride=block_cols), :]
                pieces[member(col, PLACES * c + s)] = piece.astype(pieces.dtype)
                high, low = high_low(square[pl.ds(block, 1), :])
                row = 2 * (SLOTS * c + s)
                notes[row : row + 1, :] = high
                notes[row + 1 : row + 2, :] = low

                @pl.when(held >= 0)
                def _():
                    place[0, block] = member(col, PLACES * c + s)
                    place[1, block] = col * shard_rows + row

        pieces[member(col, NOTE)] = notes[...].astype(pieces.dtype)
        return carry

    lax.fori_loop(0, COLS, column, 0)
    for copy in out:
        copy.wait()


def prepare(slots, gradient, second, after):
    block_rows, shard_rows, block_cols, lanes = gradient.shape
    block_count = block_rows * block_cols
    return pl.pallas_call(
        prepare_kernel,
        out_shape=[
            jax.ShapeDtypeStruct(second.shape, second.dtype),
            jax.ShapeDtypeStruct((COLS * RING, shard_rows, lanes), gradient.dtype),
            jax.ShapeDtypeStruct((2, block_count), jnp.int32),
        ],
        in_specs=[SMEM, HBM, HBM, ANY],
        out_specs=[HBM, VMEM, SMEM],
        scratch_shapes=[
            pltpu.VMEM(gradient.shape, gradient.dtype),
            pltpu.VMEM(second.shape, second.dtype),
            pltpu.VMEM(second.shape, second.dtype),
            pltpu.VMEM((block_count * shard_rows, lanes), jnp.float32),
            pltpu.VMEM((block_count, lanes), jnp.float32),
            pltpu.VMEM((shard_rows, lanes), jnp.float32),
            pltpu.SemaphoreType.DMA((3, CHUNKS)),
        ],
        compiler_params=limit(63),
        name="prepare",
    )(slots, gradient, second, after)


def together_kernel(columns, own, *refs):
    factors, out = refs[:PLACES], refs[PLACES]
    count = columns.shape[0]
    size = own.shape[0] * own.shape[1] // columns.shape[1]
    at_home = lax.div(lax.axis_index("replica"), PLACES) == lax.axis_index("core")
    out[:count] = columns[...]
    for step in range(1, PLACES):
        out[count + step * size : count + (step + 1) * size] = factors[step][...].reshape((size,) + columns.shape[1:])

    @pl.when(at_home)
    def _():
        out[count : count + size] = own[...].reshape((size,) + columns.shape[1:])

    @pl.when(jnp.logical_not(at_home))
    def _():
        out[count : count + size] = factors[0][...].reshape((size,) + columns.shape[1:])


def together(columns, own, factors):
    count, rows, part = columns.shape
    count += PLACES * own.shape[0] * own.shape[1] // rows
    return pl.pallas_call(
        together_kernel,
        out_shape=jax.ShapeDtypeStruct((count, rows, part), columns.dtype),
        in_specs=[VMEM] * (2 + PLACES),
        out_specs=VMEM,
        compiler_params=limit(16),
        name="together",
    )(columns, own, *factors)


def block_kernel(own, swapped, out, lf, rf, grad, half, full, notes):
    rows, part = own.shape[1:]
    order = lf.shape[0]
    count = COLS * RING
    groups = part // rows
    core = lax.axis_index("core")
    here = lax.axis_index("replica")
    place = lax.rem(here, PLACES)

    @pl.when(place < SLOTS)
    def _():
        owner_core = lax.div(here, PLACES)
        for b, held in enumerate((own, swapped)):
            h = core if b == 0 else 1 - core
            for col in range(COLS):
                for r in range(RING):
                    grad[col, h, :, r * part : (r + 1) * part] = held[member(col, r)]
            for step in range(PLACES):
                source = lax.rem(here + step + jnp.where(h == owner_core, 0, PLACES), RING)
                at = pl.ds(pl.multiple_of(source * part, part), part)
                for j in range(RING):
                    left = count + (2 * RING * step + j) * groups
                    right = left + RING * groups
                    lf[at, j * part : (j + 1) * part] = held[left : left + groups].reshape(part, part)
                    rf[j * part : (j + 1) * part, at] = held[right : right + groups].reshape(part, part)

        tile = 2 * part
        steps = order // tile

        def first(t, carry):
            at = pl.ds(pl.multiple_of(t * tile, tile), tile)
            rhs = grad[:, :, :, at].reshape(order, tile)
            half[:, at] = jnp.dot(lf[...], rhs, preferred_element_type=jnp.float32).astype(half.dtype)
            return carry

        lax.fori_loop(0, steps, first, 0, unroll=True)

        def second(t, square):
            at = pl.ds(pl.multiple_of(t * tile, tile), tile)
            value = jnp.dot(half[...], rf[:, at], preferred_element_type=jnp.float32)
            full[:, :, :, at] = value.reshape(COLS, CORES, rows, tile)
            return square + jnp.sum(value * value, axis=0, keepdims=True)

        square = lax.fori_loop(0, steps, second, jnp.zeros((1, tile), jnp.float32), unroll=True)
        square = jnp.sum(square, axis=1, keepdims=True)
        scale = 1.0 / jnp.sqrt(square + NORM_EPS)
        for r in range(RING):
            value = (full[:, core, :, r * part : (r + 1) * part] * scale).astype(out.dtype)
            for col in range(COLS):
                out[member(col, r)] = value[col]

    @pl.when(place == NOTE)
    def _():
        total = jnp.zeros(notes.shape, jnp.float32)
        for held in (own, swapped):
            total = total + jnp.sum(held[:count].astype(jnp.float32), axis=0)
        notes[...] = total
        for row in range(0, 2 * CORES * SLOTS, 2):
            high, low = high_low(notes[row : row + 1, :] + notes[row + 1 : row + 2, :])
            notes[row : row + 1, :] = high
            notes[row + 1 : row + 2, :] = low
        out[...] = jnp.broadcast_to(notes[...].astype(out.dtype), out.shape)


def precondition(own, swapped):
    _, rows, part = own.shape
    order = RING * part
    kind = own.dtype
    return pl.pallas_call(
        block_kernel,
        out_shape=jax.ShapeDtypeStruct((COLS * RING, rows, part), kind),
        in_specs=[VMEM] * 2,
        out_specs=VMEM,
        scratch_shapes=[
            pltpu.VMEM((order, order), kind),
            pltpu.VMEM((order, order), kind),
            pltpu.VMEM((COLS, CORES, rows, order), kind),
            pltpu.VMEM((order, order), kind),
            pltpu.VMEM((COLS, CORES, rows, order), jnp.float32),
            pltpu.VMEM((rows, part), jnp.float32),
        ],
        compiler_params=limit(28),
        cost_estimate=pl.CostEstimate(flops=4 * order**3, bytes_accessed=10 * order * order, transcendentals=0),
        name="precondition",
    )(own, swapped)


def finish_kernel(place, returned, momentum, out, wide, adam):
    block_rows, shard_rows, block_cols, lanes = momentum.shape
    for col in range(COLS):
        note = jnp.sum(returned[member(col, NOTE)].astype(jnp.float32), axis=1, keepdims=True)
        adam[col * shard_rows : (col + 1) * shard_rows, :] = jnp.broadcast_to(note, (shard_rows, lanes))

    def step(i, carry):
        for j in range(block_cols):
            block = i * block_cols + j
            row = place[1, block]
            scale = jnp.sqrt(adam[pl.ds(row, 1), :] + adam[pl.ds(row + 1, 1), :])
            piece = returned[place[0, block]].astype(jnp.float32) * scale
            wide[pl.ds(j, shard_rows, stride=block_cols), :] = piece
        grafted = wide[...].reshape(shard_rows, block_cols, lanes)
        out[i] = (BETA_ONE * momentum[i].astype(jnp.float32) + grafted).astype(out.dtype)
        return carry

    lax.fori_loop(0, block_rows, step, 0)


def finish(place, returned, momentum):
    block_rows, shard_rows, block_cols, lanes = momentum.shape
    return pl.pallas_call(
        finish_kernel,
        out_shape=jax.ShapeDtypeStruct(momentum.shape, momentum.dtype),
        in_specs=[SMEM, VMEM, VMEM],
        out_specs=VMEM,
        scratch_shapes=[
            pltpu.VMEM((shard_rows * block_cols, lanes), jnp.float32),
            pltpu.VMEM((COLS * shard_rows, lanes), jnp.float32),
        ],
        compiler_params=limit(16),
        name="finish",
    )(place, returned, momentum)


def exchange(array):
    return lax.all_to_all(array, COL + ("replica",), split_axis=0, concat_axis=0, tiled=True)


def swap(array):
    return lax.ppermute(array, "core", [(0, 1), (1, 0)])


def local(gradient, second_moment, momentum, left_factor, right_factor, block_of_slot):
    spread = spread_factors(left_factor, right_factor)
    factors = [
        lax.ppermute(shard, ("core", "replica"), factor_pairs(step)) for step, shard in enumerate(spread)
    ]
    moment_new, pieces, place = prepare(block_of_slot.T, gradient, second_moment, spread[0])
    columns = lax.cond(block_of_slot[0, 0] >= -1, exchange, jnp.zeros_like, pieces)
    held = together(columns, spread[0], factors)
    parts = precondition(held, swap(held))
    return (finish(place, exchange(parts), momentum), moment_new)


def solution(mesh):
    fine = Mesh(mesh.devices.reshape(SHAPE), COL + ("core", "replica"))
    fsdp = COL + ("core",)
    in_specs = (
        P(None, fsdp, None, "replica"),
        P(None, fsdp, None, "replica"),
        P(None, fsdp, None, "replica"),
        P(fsdp, "replica", None),
        P(fsdp, None, "replica"),
        P(),
    )
    out_specs = (P(None, fsdp, None, "replica"), P(None, fsdp, None, "replica"))
    return jax.shard_map(local, mesh=fine, in_specs=in_specs, out_specs=out_specs, check_vma=False)
```

```python
import jax
import jax.numpy as jnp
from jax import lax
from jax.experimental import pallas as pl
from jax.experimental.pallas import tpu as pltpu
from jax.sharding import Mesh
from jax.sharding import PartitionSpec as P

BETA_ONE = 0.9
BETA_TWO = 0.999
ADAM_EPS = 1e-08
NORM_EPS = 1e-06

RING = 8
COLS = 32
SLOTS = 3
PLACES = 4
CORES = 2
NOTE = 3
CHUNKS = 4
DIRECT = 2

ANY = pl.BlockSpec(memory_space=pl.ANY)
HBM = pl.BlockSpec(memory_space=pltpu.HBM)
VMEM = pl.BlockSpec(memory_space=pltpu.VMEM)
SMEM = pl.BlockSpec(memory_space=pltpu.SMEM)


def limit(mebibytes):
    return pltpu.CompilerParams(vmem_limit_bytes=mebibytes * 1024 * 1024)


def high_low(value):
    high = value.astype(jnp.bfloat16).astype(jnp.float32)
    return high, value - high


def member(col, place):
    return col * RING + place


def factor_pairs(step):
    pairs = []
    for c in range(CORES):
        for s in range(SLOTS):
            root = PLACES * c + s
            near, far = (root + step) % RING, (root + step + PLACES) % RING
            if step > 0:
                pairs.append((c * RING + near, c * RING + root))
                pairs.append((c * RING + far, (1 - c) * RING + root))
            elif s == DIRECT:
                pairs.append((c * RING + far, (1 - c) * RING + root))
            else:
                pairs.append((c * RING + far, c * RING + root + 1))
    return pairs


def relay_pairs():
    pairs = []
    for c in range(CORES):
        for s in range(SLOTS):
            root = PLACES * c + s
            if s != DIRECT:
                pairs.append((c * RING + root + 1, (1 - c) * RING + root))
    return pairs


def factor_kernel(left, right, *refs):
    outs, held_left, held_right, sems = refs[:PLACES], *refs[PLACES:]
    part = left.shape[1]
    here = lax.axis_index("replica")
    copies = []
    for s in range(SLOTS):
        copies.append(pltpu.make_async_copy(left.at[s], held_left.at[s], sems.at[0, s]))
        copies.append(pltpu.make_async_copy(right.at[s], held_right.at[s], sems.at[1, s]))
    for copy in copies:
        copy.start()
    for copy in copies:
        copy.wait()
    for step in range(PLACES):
        slot = lax.rem(here - step + RING, PLACES)

        @pl.when(slot < SLOTS)
        def _():
            for j in range(RING):
                outs[step][j] = held_left[slot, :, j * part : (j + 1) * part]
                outs[step][RING + j] = held_right[slot, j * part : (j + 1) * part, :]


def spread_factors(left, right):
    part = left.shape[1]
    return pl.pallas_call(
        factor_kernel,
        out_shape=[jax.ShapeDtypeStruct((2 * RING, part, part), left.dtype)] * PLACES,
        in_specs=[HBM, HBM],
        out_specs=[VMEM] * PLACES,
        scratch_shapes=[
            pltpu.VMEM(left.shape, left.dtype),
            pltpu.VMEM(right.shape, right.dtype),
            pltpu.SemaphoreType.DMA((2, SLOTS)),
        ],
        compiler_params=limit(63),
        name="spread_factors",
    )(left, right)


def prepare_kernel(slots, gradient, second, after, moment, pieces, place, *scratch):
    held_gradient, held_second, held_moment, wide, square, notes, sems = scratch
    block_rows, shard_rows, block_cols, lanes = gradient.shape
    per_row = shard_rows * block_cols
    chunk = block_rows // CHUNKS
    chunks = [pl.ds(at * chunk, chunk) for at in range(CHUNKS)]
    first, second_in, out = [], [], []
    for at, rows in enumerate(chunks):
        first.append(pltpu.make_async_copy(gradient.at[rows], held_gradient.at[rows], sems.at[0, at]))
        second_in.append(pltpu.make_async_copy(second.at[rows], held_second.at[rows], sems.at[1, at]))
        out.append(pltpu.make_async_copy(held_moment.at[rows], moment.at[rows], sems.at[2, at]))
        first[at].start()
        second_in[at].start()

    def adam(i, carry):
        g = held_gradient[i].astype(jnp.float32)
        v = BETA_TWO * held_second[i].astype(jnp.float32) + (1.0 - BETA_TWO) * g * g
        held_moment[i] = v.astype(moment.dtype)
        step = g / (jnp.sqrt(v) + ADAM_EPS)
        square[pl.ds(pl.multiple_of(i * block_cols, block_cols), block_cols), :] = jnp.sum(step * step, axis=0)
        wide[pl.ds(pl.multiple_of(i * per_row, per_row), per_row), :] = g.reshape(per_row, lanes)
        return carry

    for at in range(CHUNKS):
        first[at].wait()
        second_in[at].wait()
        lax.fori_loop(at * chunk, (at + 1) * chunk, adam, 0)
        out[at].start()
    notes[...] = jnp.zeros(notes.shape, notes.dtype)

    def column(col, carry):
        for c in range(CORES):
            for s in range(SLOTS):
                held = slots[s, col * CORES + c]
                block = jnp.maximum(held, 0)
                i = lax.div(block, block_cols)
                j = lax.rem(block, block_cols)
                piece = wide[pl.ds(i * per_row + j, shard_rows, stride=block_cols), :]
                pieces[member(col, PLACES * c + s)] = piece.astype(pieces.dtype)
                high, low = high_low(square[pl.ds(block, 1), :])
                row = 2 * (SLOTS * c + s)
                notes[row : row + 1, :] = high
                notes[row + 1 : row + 2, :] = low

                @pl.when(held >= 0)
                def _():
                    place[0, block] = member(col, PLACES * c + s)
                    place[1, block] = col * shard_rows + row

        pieces[member(col, NOTE)] = notes[...].astype(pieces.dtype)
        return carry

    lax.fori_loop(0, COLS, column, 0)
    for copy in out:
        copy.wait()


def prepare(slots, gradient, second, after):
    block_rows, shard_rows, block_cols, lanes = gradient.shape
    block_count = block_rows * block_cols
    return pl.pallas_call(
        prepare_kernel,
        out_shape=[
            jax.ShapeDtypeStruct(second.shape, second.dtype),
            jax.ShapeDtypeStruct((COLS * RING, shard_rows, lanes), gradient.dtype),
            jax.ShapeDtypeStruct((2, block_count), jnp.int32),
        ],
        in_specs=[SMEM, HBM, HBM, ANY],
        out_specs=[HBM, VMEM, SMEM],
        scratch_shapes=[
            pltpu.VMEM(gradient.shape, gradient.dtype),
            pltpu.VMEM(second.shape, second.dtype),
            pltpu.VMEM(second.shape, second.dtype),
            pltpu.VMEM((block_count * shard_rows, lanes), jnp.float32),
            pltpu.VMEM((block_count, lanes), jnp.float32),
            pltpu.VMEM((shard_rows, lanes), jnp.float32),
            pltpu.SemaphoreType.DMA((3, CHUNKS)),
        ],
        compiler_params=limit(63),
        name="prepare",
    )(slots, gradient, second, after)


def released_kernel(*refs):
    pass


def released(array, other):
    return pl.pallas_call(
        released_kernel,
        out_shape=jax.ShapeDtypeStruct(array.shape, array.dtype),
        in_specs=[ANY, ANY],
        out_specs=ANY,
        input_output_aliases={0: 0},
        name="released",
    )(array, other)


def together_kernel(columns, own, relayed, *refs):
    factors, out = refs[:PLACES], refs[PLACES]
    count, rows, part = columns.shape
    size = own.shape[0] * own.shape[1] // rows
    here = lax.axis_index("replica")
    at_home = lax.div(here, PLACES) == lax.axis_index("core")
    direct = lax.rem(here, PLACES) == DIRECT
    out[:count] = columns[...]
    for step in range(1, PLACES):
        out[count + step * size : count + (step + 1) * size] = factors[step][...].reshape(size, rows, part)

    @pl.when(at_home)
    def _():
        out[count : count + size] = own[...].reshape(size, rows, part)

    @pl.when(jnp.logical_not(at_home) & direct)
    def _():
        out[count : count + size] = factors[0][...].reshape(size, rows, part)

    @pl.when(jnp.logical_not(at_home) & jnp.logical_not(direct))
    def _():
        out[count : count + size] = relayed[...].reshape(size, rows, part)


def together(columns, shards):
    count, rows, part = columns.shape
    count += PLACES * shards[0].shape[0] * shards[0].shape[1] // rows
    return pl.pallas_call(
        together_kernel,
        out_shape=jax.ShapeDtypeStruct((count, rows, part), columns.dtype),
        in_specs=[VMEM] * (1 + len(shards)),
        out_specs=VMEM,
        compiler_params=limit(16),
        name="together",
    )(columns, *shards)


def block_kernel(own, swapped, out, lf, rf, grad, half, full, notes):
    rows, part = own.shape[1:]
    order = lf.shape[0]
    count = COLS * RING
    groups = part // rows
    core = lax.axis_index("core")
    here = lax.axis_index("replica")
    place = lax.rem(here, PLACES)

    @pl.when(place < SLOTS)
    def _():
        owner_core = lax.div(here, PLACES)
        for b, held in enumerate((own, swapped)):
            h = core if b == 0 else 1 - core
            for col in range(COLS):
                for r in range(RING):
                    grad[col, h, :, r * part : (r + 1) * part] = held[member(col, r)]
            for step in range(PLACES):
                source = lax.rem(here + step + jnp.where(h == owner_core, 0, PLACES), RING)
                at = pl.ds(pl.multiple_of(source * part, part), part)
                for j in range(RING):
                    left = count + (2 * RING * step + j) * groups
                    right = left + RING * groups
                    lf[at, j * part : (j + 1) * part] = held[left : left + groups].reshape(part, part)
                    rf[j * part : (j + 1) * part, at] = held[right : right + groups].reshape(part, part)

        tile = 2 * part
        steps = order // tile

        def first(t, carry):
            at = pl.ds(pl.multiple_of(t * tile, tile), tile)
            rhs = grad[:, :, :, at].reshape(order, tile)
            half[:, at] = jnp.dot(lf[...], rhs, preferred_element_type=jnp.float32).astype(half.dtype)
            return carry

        lax.fori_loop(0, steps, first, 0, unroll=True)

        def second(t, square):
            at = pl.ds(pl.multiple_of(t * tile, tile), tile)
            value = jnp.dot(half[...], rf[:, at], preferred_element_type=jnp.float32)
            full[:, :, :, at] = value.reshape(COLS, CORES, rows, tile)
            return square + jnp.sum(value * value, axis=0, keepdims=True)

        square = lax.fori_loop(0, steps, second, jnp.zeros((1, tile), jnp.float32), unroll=True)
        square = jnp.sum(square, axis=1, keepdims=True)
        scale = 1.0 / jnp.sqrt(square + NORM_EPS)
        for r in range(RING):
            value = (full[:, core, :, r * part : (r + 1) * part] * scale).astype(out.dtype)
            for col in range(COLS):
                out[member(col, r)] = value[col]

    @pl.when(place == NOTE)
    def _():
        total = jnp.zeros(notes.shape, jnp.float32)
        for held in (own, swapped):
            total = total + jnp.sum(held[:count].astype(jnp.float32), axis=0)
        notes[...] = total
        for row in range(0, 2 * CORES * SLOTS, 2):
            high, low = high_low(notes[row : row + 1, :] + notes[row + 1 : row + 2, :])
            notes[row : row + 1, :] = high
            notes[row + 1 : row + 2, :] = low
        out[...] = jnp.broadcast_to(notes[...].astype(out.dtype), out.shape)


def precondition(own, swapped):
    _, rows, part = own.shape
    order = RING * part
    kind = own.dtype
    return pl.pallas_call(
        block_kernel,
        out_shape=jax.ShapeDtypeStruct((COLS * RING, rows, part), kind),
        in_specs=[VMEM] * 2,
        out_specs=VMEM,
        scratch_shapes=[
            pltpu.VMEM((order, order), kind),
            pltpu.VMEM((order, order), kind),
            pltpu.VMEM((COLS, CORES, rows, order), kind),
            pltpu.VMEM((order, order), kind),
            pltpu.VMEM((COLS, CORES, rows, order), jnp.float32),
            pltpu.VMEM((rows, part), jnp.float32),
        ],
        compiler_params=limit(28),
        cost_estimate=pl.CostEstimate(flops=4 * order**3, bytes_accessed=10 * order * order, transcendentals=0),
        name="precondition",
    )(own, swapped)


def finish_kernel(place, returned, momentum, out, wide, adam):
    block_rows, shard_rows, block_cols, lanes = momentum.shape
    for col in range(COLS):
        note = jnp.sum(returned[member(col, NOTE)].astype(jnp.float32), axis=1, keepdims=True)
        adam[col * shard_rows : (col + 1) * shard_rows, :] = jnp.broadcast_to(note, (shard_rows, lanes))

    def step(i, carry):
        for j in range(block_cols):
            block = i * block_cols + j
            row = place[1, block]
            scale = jnp.sqrt(adam[pl.ds(row, 1), :] + adam[pl.ds(row + 1, 1), :])
            piece = returned[place[0, block]].astype(jnp.float32) * scale
            wide[pl.ds(j, shard_rows, stride=block_cols), :] = piece
        grafted = wide[...].reshape(shard_rows, block_cols, lanes)
        out[i] = (BETA_ONE * momentum[i].astype(jnp.float32) + grafted).astype(out.dtype)
        return carry

    lax.fori_loop(0, block_rows, step, 0)


def finish(place, returned, momentum):
    block_rows, shard_rows, block_cols, lanes = momentum.shape
    return pl.pallas_call(
        finish_kernel,
        out_shape=jax.ShapeDtypeStruct(momentum.shape, momentum.dtype),
        in_specs=[SMEM, VMEM, VMEM],
        out_specs=VMEM,
        scratch_shapes=[
            pltpu.VMEM((shard_rows * block_cols, lanes), jnp.float32),
            pltpu.VMEM((COLS * shard_rows, lanes), jnp.float32),
        ],
        compiler_params=limit(16),
        name="finish",
    )(place, returned, momentum)


def exchange(array):
    return lax.all_to_all(array, ("col", "replica"), split_axis=0, concat_axis=0, tiled=True)


def swap(array):
    return lax.ppermute(array, "core", [(0, 1), (1, 0)])


def local(gradient, second_moment, momentum, left_factor, right_factor, block_of_slot):
    spread = spread_factors(left_factor, right_factor)
    line = ("core", "replica")
    factors = [lax.ppermute(shard, line, factor_pairs(step)) for step, shard in enumerate(spread)]

    moment_new, pieces, place = prepare(block_of_slot.T, gradient, second_moment, spread[0])
    factors[0] = released(factors[0], pieces)
    relayed = lax.ppermute(factors[0], line, relay_pairs())
    columns = lax.cond(lax.axis_index("core") < CORES, exchange, jnp.zeros_like, pieces)
    held = together(columns, [spread[0], relayed] + factors)
    parts = precondition(held, swap(held))
    return (finish(place, exchange(parts), momentum), moment_new)


def solution(mesh):
    fine = Mesh(mesh.devices.reshape(COLS, CORES, RING), ("col", "core", "replica"))
    fsdp = ("col", "core")
    in_specs = (
        P(None, fsdp, None, "replica"),
        P(None, fsdp, None, "replica"),
        P(None, fsdp, None, "replica"),
        P(fsdp, "replica", None),
        P(fsdp, None, "replica"),
        P(),
    )
    out_specs = (P(None, fsdp, None, "replica"), P(None, fsdp, None, "replica"))
    return jax.shard_map(local, mesh=fine, in_specs=in_specs, out_specs=out_specs, check_vma=False)
```

```python
import jax
import jax.numpy as jnp
from jax import lax
from jax.experimental import pallas as pl
from jax.experimental.pallas import tpu as pltpu
from jax.sharding import Mesh
from jax.sharding import PartitionSpec as P

BETA_ONE = 0.9
BETA_TWO = 0.999
ADAM_EPS = 1e-08
NORM_EPS = 1e-06

RING = 8
COLS = 32
SLOTS = 3
PLACES = 4
CORES = 2
NOTE = 3
CHUNKS = 4
DIRECT = 2
EARLY = 2

ANY = pl.BlockSpec(memory_space=pl.ANY)
HBM = pl.BlockSpec(memory_space=pltpu.HBM)
VMEM = pl.BlockSpec(memory_space=pltpu.VMEM)
SMEM = pl.BlockSpec(memory_space=pltpu.SMEM)


def limit(mebibytes):
    return pltpu.CompilerParams(vmem_limit_bytes=mebibytes * 1024 * 1024)


def high_low(value):
    high = value.astype(jnp.bfloat16).astype(jnp.float32)
    return high, value - high


def member(col, place):
    return col * RING + place


def factor_pairs(step):
    pairs = []
    for c in range(CORES):
        for s in range(SLOTS):
            root = PLACES * c + s
            near, far = (root + step) % RING, (root + step + PLACES) % RING
            if step > 0:
                pairs.append((c * RING + near, c * RING + root))
                pairs.append((c * RING + far, (1 - c) * RING + root))
            elif s == DIRECT:
                pairs.append((c * RING + far, (1 - c) * RING + root))
            else:
                pairs.append((c * RING + far, c * RING + root + 1))
    return pairs


def relay_pairs():
    pairs = []
    for c in range(CORES):
        for s in range(SLOTS):
            root = PLACES * c + s
            if s != DIRECT:
                pairs.append((c * RING + root + 1, (1 - c) * RING + root))
    return pairs


def factor_kernel(left, right, *refs):
    outs, held_left, held_right, sems = refs[:PLACES], *refs[PLACES:]
    part = left.shape[1]
    here = lax.axis_index("replica")
    copies = []
    for s in range(SLOTS):
        copies.append(pltpu.make_async_copy(left.at[s], held_left.at[s], sems.at[0, s]))
        copies.append(pltpu.make_async_copy(right.at[s], held_right.at[s], sems.at[1, s]))
    for copy in copies:
        copy.start()
    for copy in copies:
        copy.wait()
    for step in range(PLACES):
        slot = lax.rem(here - step + RING, PLACES)

        @pl.when(slot < SLOTS)
        def _():
            for j in range(RING):
                outs[step][j] = held_left[slot, :, j * part : (j + 1) * part]
                outs[step][RING + j] = held_right[slot, j * part : (j + 1) * part, :]


def spread_factors(left, right):
    part = left.shape[1]
    return pl.pallas_call(
        factor_kernel,
        out_shape=[jax.ShapeDtypeStruct((2 * RING, part, part), left.dtype)] * PLACES,
        in_specs=[HBM, HBM],
        out_specs=[VMEM] * PLACES,
        scratch_shapes=[
            pltpu.VMEM(left.shape, left.dtype),
            pltpu.VMEM(right.shape, right.dtype),
            pltpu.SemaphoreType.DMA((2, SLOTS)),
        ],
        compiler_params=limit(63),
        name="spread_factors",
    )(left, right)


def prepare_kernel(slots, gradient, second, after, moment, pieces, place, *scratch):
    held_gradient, held_second, held_moment, wide, square, notes, sems = scratch
    block_rows, shard_rows, block_cols, lanes = gradient.shape
    per_row = shard_rows * block_cols
    chunk = block_rows // CHUNKS
    chunks = [pl.ds(at * chunk, chunk) for at in range(CHUNKS)]
    first, second_in, out = [], [], []
    for at, rows in enumerate(chunks):
        first.append(pltpu.make_async_copy(gradient.at[rows], held_gradient.at[rows], sems.at[0, at]))
        second_in.append(pltpu.make_async_copy(second.at[rows], held_second.at[rows], sems.at[1, at]))
        out.append(pltpu.make_async_copy(held_moment.at[rows], moment.at[rows], sems.at[2, at]))
        first[at].start()
        second_in[at].start()

    def adam(i, carry):
        g = held_gradient[i].astype(jnp.float32)
        v = BETA_TWO * held_second[i].astype(jnp.float32) + (1.0 - BETA_TWO) * g * g
        held_moment[i] = v.astype(moment.dtype)
        step = g / (jnp.sqrt(v) + ADAM_EPS)
        square[pl.ds(pl.multiple_of(i * block_cols, block_cols), block_cols), :] = jnp.sum(step * step, axis=0)
        wide[pl.ds(pl.multiple_of(i * per_row, per_row), per_row), :] = g.reshape(per_row, lanes)
        return carry

    for at in range(CHUNKS):
        first[at].wait()
        second_in[at].wait()
        lax.fori_loop(at * chunk, (at + 1) * chunk, adam, 0)
        out[at].start()
    notes[...] = jnp.zeros(notes.shape, notes.dtype)

    def column(col, carry):
        for c in range(CORES):
            for s in range(SLOTS):
                held = slots[s, col * CORES + c]
                block = jnp.maximum(held, 0)
                i = lax.div(block, block_cols)
                j = lax.rem(block, block_cols)
                piece = wide[pl.ds(i * per_row + j, shard_rows, stride=block_cols), :]
                pieces[member(col, PLACES * c + s)] = piece.astype(pieces.dtype)
                high, low = high_low(square[pl.ds(block, 1), :])
                row = 2 * (SLOTS * c + s)
                notes[row : row + 1, :] = high
                notes[row + 1 : row + 2, :] = low

                @pl.when(held >= 0)
                def _():
                    place[0, block] = member(col, PLACES * c + s)
                    place[1, block] = col * shard_rows + row

        pieces[member(col, NOTE)] = notes[...].astype(pieces.dtype)
        return carry

    lax.fori_loop(0, COLS, column, 0)
    for copy in out:
        copy.wait()


def prepare(slots, gradient, second, after):
    block_rows, shard_rows, block_cols, lanes = gradient.shape
    block_count = block_rows * block_cols
    return pl.pallas_call(
        prepare_kernel,
        out_shape=[
            jax.ShapeDtypeStruct(second.shape, second.dtype),
            jax.ShapeDtypeStruct((COLS * RING, shard_rows, lanes), gradient.dtype),
            jax.ShapeDtypeStruct((2, block_count), jnp.int32),
        ],
        in_specs=[SMEM, HBM, HBM, ANY],
        out_specs=[HBM, VMEM, SMEM],
        scratch_shapes=[
            pltpu.VMEM(gradient.shape, gradient.dtype),
            pltpu.VMEM(second.shape, second.dtype),
            pltpu.VMEM(second.shape, second.dtype),
            pltpu.VMEM((block_count * shard_rows, lanes), jnp.float32),
            pltpu.VMEM((block_count, lanes), jnp.float32),
            pltpu.VMEM((shard_rows, lanes), jnp.float32),
            pltpu.SemaphoreType.DMA((3, CHUNKS)),
        ],
        compiler_params=limit(63),
        name="prepare",
    )(slots, gradient, second, after)


def released_kernel(*refs):
    pass


def released(arrays, other):
    count = len(arrays)
    return pl.pallas_call(
        released_kernel,
        out_shape=[jax.ShapeDtypeStruct(array.shape, array.dtype) for array in arrays],
        in_specs=[ANY] * (count + 1),
        out_specs=[ANY] * count,
        input_output_aliases={at: at for at in range(count)},
        compiler_params=limit(63),
        name="released",
    )(*arrays, other)


def together_kernel(columns, own, relayed, *refs):
    factors, out = refs[:PLACES], refs[PLACES]
    count, rows, part = columns.shape
    size = own.shape[0] * own.shape[1] // rows
    here = lax.axis_index("replica")
    at_home = lax.div(here, PLACES) == lax.axis_index("core")
    direct = lax.rem(here, PLACES) == DIRECT
    out[:count] = columns[...]
    for step in range(1, PLACES):
        out[count + step * size : count + (step + 1) * size] = factors[step][...].reshape(size, rows, part)

    @pl.when(at_home)
    def _():
        out[count : count + size] = own[...].reshape(size, rows, part)

    @pl.when(jnp.logical_not(at_home) & direct)
    def _():
        out[count : count + size] = factors[0][...].reshape(size, rows, part)

    @pl.when(jnp.logical_not(at_home) & jnp.logical_not(direct))
    def _():
        out[count : count + size] = relayed[...].reshape(size, rows, part)


def together(columns, shards):
    count, rows, part = columns.shape
    count += PLACES * shards[0].shape[0] * shards[0].shape[1] // rows
    return pl.pallas_call(
        together_kernel,
        out_shape=jax.ShapeDtypeStruct((count, rows, part), columns.dtype),
        in_specs=[VMEM] * (1 + len(shards)),
        out_specs=VMEM,
        compiler_params=limit(16),
        name="together",
    )(columns, *shards)


def block_kernel(own, swapped, out, lf, rf, grad, half, full, notes):
    rows, part = own.shape[1:]
    order = lf.shape[0]
    count = COLS * RING
    groups = part // rows
    core = lax.axis_index("core")
    here = lax.axis_index("replica")
    place = lax.rem(here, PLACES)

    @pl.when(place < SLOTS)
    def _():
        owner_core = lax.div(here, PLACES)
        for b, held in enumerate((own, swapped)):
            h = core if b == 0 else 1 - core
            for col in range(COLS):
                for r in range(RING):
                    grad[col, h, :, r * part : (r + 1) * part] = held[member(col, r)]
            for step in range(PLACES):
                source = lax.rem(here + step + jnp.where(h == owner_core, 0, PLACES), RING)
                at = pl.ds(pl.multiple_of(source * part, part), part)
                for j in range(RING):
                    left = count + (2 * RING * step + j) * groups
                    right = left + RING * groups
                    lf[at, j * part : (j + 1) * part] = held[left : left + groups].reshape(part, part)
                    rf[j * part : (j + 1) * part, at] = held[right : right + groups].reshape(part, part)

        tile = 2 * part
        steps = order // tile

        def first(t, carry):
            at = pl.ds(pl.multiple_of(t * tile, tile), tile)
            rhs = grad[:, :, :, at].reshape(order, tile)
            half[:, at] = jnp.dot(lf[...], rhs, preferred_element_type=jnp.float32).astype(half.dtype)
            return carry

        lax.fori_loop(0, steps, first, 0, unroll=True)

        def second(t, square):
            at = pl.ds(pl.multiple_of(t * tile, tile), tile)
            value = jnp.dot(half[...], rf[:, at], preferred_element_type=jnp.float32)
            full[:, :, :, at] = value.reshape(COLS, CORES, rows, tile)
            return square + jnp.sum(value * value, axis=0, keepdims=True)

        square = lax.fori_loop(0, steps, second, jnp.zeros((1, tile), jnp.float32), unroll=True)
        square = jnp.sum(square, axis=1, keepdims=True)
        scale = 1.0 / jnp.sqrt(square + NORM_EPS)
        for r in range(RING):
            value = (full[:, core, :, r * part : (r + 1) * part] * scale).astype(out.dtype)
            for col in range(COLS):
                out[member(col, r)] = value[col]

    @pl.when(place == NOTE)
    def _():
        total = jnp.zeros(notes.shape, jnp.float32)
        for held in (own, swapped):
            total = total + jnp.sum(held[:count].astype(jnp.float32), axis=0)
        notes[...] = total
        for row in range(0, 2 * CORES * SLOTS, 2):
            high, low = high_low(notes[row : row + 1, :] + notes[row + 1 : row + 2, :])
            notes[row : row + 1, :] = high
            notes[row + 1 : row + 2, :] = low
        out[...] = jnp.broadcast_to(notes[...].astype(out.dtype), out.shape)


def precondition(own, swapped):
    _, rows, part = own.shape
    order = RING * part
    kind = own.dtype
    return pl.pallas_call(
        block_kernel,
        out_shape=jax.ShapeDtypeStruct((COLS * RING, rows, part), kind),
        in_specs=[VMEM] * 2,
        out_specs=VMEM,
        scratch_shapes=[
            pltpu.VMEM((order, order), kind),
            pltpu.VMEM((order, order), kind),
            pltpu.VMEM((COLS, CORES, rows, order), kind),
            pltpu.VMEM((order, order), kind),
            pltpu.VMEM((COLS, CORES, rows, order), jnp.float32),
            pltpu.VMEM((rows, part), jnp.float32),
        ],
        compiler_params=limit(28),
        cost_estimate=pl.CostEstimate(flops=4 * order**3, bytes_accessed=10 * order * order, transcendentals=0),
        name="precondition",
    )(own, swapped)


def finish_kernel(place, returned, momentum, out, wide, adam):
    block_rows, shard_rows, block_cols, lanes = momentum.shape
    for col in range(COLS):
        note = jnp.sum(returned[member(col, NOTE)].astype(jnp.float32), axis=1, keepdims=True)
        adam[col * shard_rows : (col + 1) * shard_rows, :] = jnp.broadcast_to(note, (shard_rows, lanes))

    def step(i, carry):
        for j in range(block_cols):
            block = i * block_cols + j
            row = place[1, block]
            scale = jnp.sqrt(adam[pl.ds(row, 1), :] + adam[pl.ds(row + 1, 1), :])
            piece = returned[place[0, block]].astype(jnp.float32) * scale
            wide[pl.ds(j, shard_rows, stride=block_cols), :] = piece
        grafted = wide[...].reshape(shard_rows, block_cols, lanes)
        out[i] = (BETA_ONE * momentum[i].astype(jnp.float32) + grafted).astype(out.dtype)
        return carry

    lax.fori_loop(0, block_rows, step, 0)


def finish(place, returned, momentum):
    block_rows, shard_rows, block_cols, lanes = momentum.shape
    return pl.pallas_call(
        finish_kernel,
        out_shape=jax.ShapeDtypeStruct(momentum.shape, momentum.dtype),
        in_specs=[SMEM, VMEM, VMEM],
        out_specs=VMEM,
        scratch_shapes=[
            pltpu.VMEM((shard_rows * block_cols, lanes), jnp.float32),
            pltpu.VMEM((COLS * shard_rows, lanes), jnp.float32),
        ],
        compiler_params=limit(16),
        name="finish",
    )(place, returned, momentum)


def exchange(array):
    return lax.all_to_all(array, ("col", "replica"), split_axis=0, concat_axis=0, tiled=True)


def swap(array):
    return lax.ppermute(array, "core", [(0, 1), (1, 0)])


def local(gradient, second_moment, momentum, left_factor, right_factor, block_of_slot):
    spread = spread_factors(left_factor, right_factor)
    line = ("core", "replica")
    factors = [lax.ppermute(spread[step], line, factor_pairs(step)) for step in range(EARLY)]
    moment_new, pieces, place = prepare(block_of_slot.T, gradient, second_moment, spread[0])
    later = released(spread[EARLY:], pieces)
    factors += [lax.ppermute(shard, line, factor_pairs(EARLY + at)) for at, shard in enumerate(later)]
    factors[:1] = released(factors[:1], pieces)
    relayed = lax.ppermute(factors[0], line, relay_pairs())
    columns = lax.cond(lax.axis_index("core") < CORES, exchange, jnp.zeros_like, pieces)
    held = together(columns, [spread[0], relayed] + factors)
    parts = precondition(held, swap(held))
    return (finish(place, exchange(parts), momentum), moment_new)


def solution(mesh):
    fine = Mesh(mesh.devices.reshape(COLS, CORES, RING), ("col", "core", "replica"))
    fsdp = ("col", "core")
    in_specs = (
        P(None, fsdp, None, "replica"),
        P(None, fsdp, None, "replica"),
        P(None, fsdp, None, "replica"),
        P(fsdp, "replica", None),
        P(fsdp, None, "replica"),
        P(),
    )
    out_specs = (P(None, fsdp, None, "replica"), P(None, fsdp, None, "replica"))
    return jax.shard_map(local, mesh=fine, in_specs=in_specs, out_specs=out_specs, check_vma=False)
```

```python
import jax
import jax.numpy as jnp
from jax import lax
from jax.experimental import pallas as pl
from jax.experimental.pallas import tpu as pltpu
from jax.sharding import Mesh
from jax.sharding import PartitionSpec as P

BETA_ONE = 0.9
BETA_TWO = 0.999
ADAM_EPS = 1e-08
NORM_EPS = 1e-06

RING = 8
COLS = 32
SLOTS = 3
PLACES = 4
CORES = 2
NOTE = 3
CHUNKS = 4
DIRECT = 2

ANY = pl.BlockSpec(memory_space=pl.ANY)
HBM = pl.BlockSpec(memory_space=pltpu.HBM)
VMEM = pl.BlockSpec(memory_space=pltpu.VMEM)
SMEM = pl.BlockSpec(memory_space=pltpu.SMEM)


def limit(mebibytes):
    return pltpu.CompilerParams(vmem_limit_bytes=mebibytes * 1024 * 1024)


def high_low(value):
    high = value.astype(jnp.bfloat16).astype(jnp.float32)
    return high, value - high


def member(col, place):
    return col * RING + place


def factor_pairs(step):
    pairs = []
    for c in range(CORES):
        for s in range(SLOTS):
            root = PLACES * c + s
            near, far = (root + step) % RING, (root + step + PLACES) % RING
            if step > 0:
                pairs.append((c * RING + near, c * RING + root))
                pairs.append((c * RING + far, (1 - c) * RING + root))
            elif s == DIRECT:
                pairs.append((c * RING + far, (1 - c) * RING + root))
            else:
                pairs.append((c * RING + far, c * RING + root + 1))
    return pairs


def relay_pairs():
    pairs = []
    for c in range(CORES):
        for s in range(SLOTS):
            root = PLACES * c + s
            if s != DIRECT:
                pairs.append((c * RING + root + 1, (1 - c) * RING + root))
    return pairs


def prepare_kernel(slots, gradient, second, left, right, moment, pieces_out, place, *rest):
    spread_out, held_gradient, held_second, held_moment = rest[:PLACES], *rest[PLACES : PLACES + 3]
    held_left, held_right, spread, pieces, wide, square, notes, sems, factor_sems = rest[PLACES + 3 :]
    block_rows, shard_rows, block_cols, lanes = gradient.shape
    part = left.shape[1]
    per_row = shard_rows * block_cols
    chunk = block_rows // CHUNKS
    factor_in, first, second_in, moment_copies, piece_copies = [], [], [], [], []
    for s in range(SLOTS):
        factor_in.append(pltpu.make_async_copy(left.at[s], held_left.at[s], factor_sems.at[0, s]))
        factor_in.append(pltpu.make_async_copy(right.at[s], held_right.at[s], factor_sems.at[1, s]))
    for at in range(CHUNKS):
        rows = pl.ds(at * chunk, chunk)
        first.append(pltpu.make_async_copy(gradient.at[rows], held_gradient.at[rows], sems.at[0, at]))
        second_in.append(pltpu.make_async_copy(second.at[rows], held_second.at[rows], sems.at[1, at]))
        moment_copies.append(pltpu.make_async_copy(held_moment.at[rows], moment.at[rows], sems.at[2, at]))
        group = pl.ds(at * (COLS * RING // CHUNKS), COLS * RING // CHUNKS)
        piece_copies.append(pltpu.make_async_copy(pieces.at[group], pieces_out.at[group], sems.at[3, at]))
    for copy in factor_in + first + second_in:
        copy.start()

    spread_copies = [
        pltpu.make_async_copy(spread.at[step], spread_out[step], factor_sems.at[2, step]) for step in range(PLACES)
    ]
    here = lax.axis_index("replica")
    for copy in factor_in:
        copy.wait()
    for step in range(PLACES):
        slot = lax.rem(here - step + RING, PLACES)

        @pl.when(slot < SLOTS)
        def _():
            for j in range(RING):
                spread[step, j] = held_left[slot, :, j * part : (j + 1) * part]
                spread[step, RING + j] = held_right[slot, j * part : (j + 1) * part, :]
            spread_copies[step].start()

    def adam(i, carry):
        g = held_gradient[i].astype(jnp.float32)
        v = BETA_TWO * held_second[i].astype(jnp.float32) + (1.0 - BETA_TWO) * g * g
        held_moment[i] = v.astype(moment.dtype)
        step = g / (jnp.sqrt(v) + ADAM_EPS)
        square[pl.ds(pl.multiple_of(i * block_cols, block_cols), block_cols), :] = jnp.sum(step * step, axis=0)
        wide[pl.ds(pl.multiple_of(i * per_row, per_row), per_row), :] = g.reshape(per_row, lanes)
        return carry

    for at in range(CHUNKS):
        first[at].wait()
        second_in[at].wait()
        lax.fori_loop(at * chunk, (at + 1) * chunk, adam, 0)
        moment_copies[at].start()
    notes[...] = jnp.zeros(notes.shape, notes.dtype)

    def column(col, carry):
        for c in range(CORES):
            for s in range(SLOTS):
                held = slots[s, col * CORES + c]
                block = jnp.maximum(held, 0)
                i = lax.div(block, block_cols)
                j = lax.rem(block, block_cols)
                piece = wide[pl.ds(i * per_row + j, shard_rows, stride=block_cols), :]
                pieces[member(col, PLACES * c + s)] = piece.astype(pieces.dtype)
                high, low = high_low(square[pl.ds(block, 1), :])
                row = 2 * (SLOTS * c + s)
                notes[row : row + 1, :] = high
                notes[row + 1 : row + 2, :] = low

                @pl.when(held >= 0)
                def _():
                    place[0, block] = member(col, PLACES * c + s)
                    place[1, block] = col * shard_rows + row

        pieces[member(col, NOTE)] = notes[...].astype(pieces.dtype)
        return carry

    for at in range(CHUNKS):
        lax.fori_loop(at * (COLS // CHUNKS), (at + 1) * (COLS // CHUNKS), column, 0)
        piece_copies[at].start()
    for step in range(PLACES):
        slot = lax.rem(here - step + RING, PLACES)

        @pl.when(slot < SLOTS)
        def _():
            spread_copies[step].wait()

    for copy in moment_copies + piece_copies:
        copy.wait()


def prepare(slots, gradient, second, left, right):
    block_rows, shard_rows, block_cols, lanes = gradient.shape
    block_count = block_rows * block_cols
    part = left.shape[1]
    kind = gradient.dtype
    dma = pltpu.SemaphoreType.DMA
    return pl.pallas_call(
        prepare_kernel,
        out_shape=[
            jax.ShapeDtypeStruct(second.shape, second.dtype),
            jax.ShapeDtypeStruct((COLS * RING, shard_rows, lanes), kind),
            jax.ShapeDtypeStruct((2, block_count), jnp.int32),
        ]
        + [jax.ShapeDtypeStruct((2 * RING, part, part), left.dtype)] * PLACES,
        in_specs=[SMEM] + [HBM] * 4,
        out_specs=[HBM, HBM, SMEM] + [HBM] * PLACES,
        scratch_shapes=[
            pltpu.VMEM(gradient.shape, kind),
            pltpu.VMEM(second.shape, second.dtype),
            pltpu.VMEM(second.shape, second.dtype),
            pltpu.VMEM(left.shape, left.dtype),
            pltpu.VMEM(right.shape, right.dtype),
            pltpu.VMEM((PLACES, 2 * RING, part, part), left.dtype),
            pltpu.VMEM((COLS * RING, shard_rows, lanes), kind),
            pltpu.VMEM((block_count * shard_rows, lanes), jnp.float32),
            pltpu.VMEM((block_count, lanes), jnp.float32),
            pltpu.VMEM((shard_rows, lanes), jnp.float32),
            dma((4, CHUNKS)),
            dma((3, PLACES)),
        ],
        compiler_params=limit(63),
        name="prepare",
    )(slots, gradient, second, left, right)


def together_kernel(columns, own, relayed, *refs):
    factors, out = refs[:PLACES], refs[PLACES]
    count, rows, part = columns.shape
    size = own.shape[0] * own.shape[1] // rows
    here = lax.axis_index("replica")
    at_home = lax.div(here, PLACES) == lax.axis_index("core")
    direct = lax.rem(here, PLACES) == DIRECT
    out[:count] = columns[...]
    for step in range(1, PLACES):
        out[count + step * size : count + (step + 1) * size] = factors[step][...].reshape(size, rows, part)

    @pl.when(at_home)
    def _():
        out[count : count + size] = own[...].reshape(size, rows, part)

    @pl.when(jnp.logical_not(at_home) & direct)
    def _():
        out[count : count + size] = factors[0][...].reshape(size, rows, part)

    @pl.when(jnp.logical_not(at_home) & jnp.logical_not(direct))
    def _():
        out[count : count + size] = relayed[...].reshape(size, rows, part)


def together(columns, shards):
    count, rows, part = columns.shape
    count += PLACES * shards[0].shape[0] * shards[0].shape[1] // rows
    return pl.pallas_call(
        together_kernel,
        out_shape=jax.ShapeDtypeStruct((count, rows, part), columns.dtype),
        in_specs=[VMEM] * (1 + len(shards)),
        out_specs=VMEM,
        compiler_params=limit(16),
        name="together",
    )(columns, *shards)


def block_kernel(own, swapped, out, lf, rf, grad, half, full, notes):
    rows, part = own.shape[1:]
    order = lf.shape[0]
    count = COLS * RING
    groups = part // rows
    core = lax.axis_index("core")
    here = lax.axis_index("replica")
    place = lax.rem(here, PLACES)

    @pl.when(place < SLOTS)
    def _():
        owner_core = lax.div(here, PLACES)
        for b, held in enumerate((own, swapped)):
            h = core if b == 0 else 1 - core
            for col in range(COLS):
                for r in range(RING):
                    grad[col, h, :, r * part : (r + 1) * part] = held[member(col, r)]
            for step in range(PLACES):
                source = lax.rem(here + step + jnp.where(h == owner_core, 0, PLACES), RING)
                at = pl.ds(pl.multiple_of(source * part, part), part)
                for j in range(RING):
                    left = count + (2 * RING * step + j) * groups
                    right = left + RING * groups
                    lf[at, j * part : (j + 1) * part] = held[left : left + groups].reshape(part, part)
                    rf[j * part : (j + 1) * part, at] = held[right : right + groups].reshape(part, part)

        tile = 2 * part
        steps = order // tile

        def first(t, carry):
            at = pl.ds(pl.multiple_of(t * tile, tile), tile)
            rhs = grad[:, :, :, at].reshape(order, tile)
            half[:, at] = jnp.dot(lf[...], rhs, preferred_element_type=jnp.float32).astype(half.dtype)
            return carry

        lax.fori_loop(0, steps, first, 0, unroll=True)

        def second(t, square):
            at = pl.ds(pl.multiple_of(t * tile, tile), tile)
            value = jnp.dot(half[...], rf[:, at], preferred_element_type=jnp.float32)
            full[:, :, :, at] = value.reshape(COLS, CORES, rows, tile)
            return square + jnp.sum(value * value, axis=0, keepdims=True)

        square = lax.fori_loop(0, steps, second, jnp.zeros((1, tile), jnp.float32), unroll=True)
        square = jnp.sum(square, axis=1, keepdims=True)
        scale = 1.0 / jnp.sqrt(square + NORM_EPS)
        for r in range(RING):
            value = (full[:, core, :, r * part : (r + 1) * part] * scale).astype(out.dtype)
            for col in range(COLS):
                out[member(col, r)] = value[col]

    @pl.when(place == NOTE)
    def _():
        total = jnp.zeros(notes.shape, jnp.float32)
        for held in (own, swapped):
            total = total + jnp.sum(held[:count].astype(jnp.float32), axis=0)
        notes[...] = total
        for row in range(0, 2 * CORES * SLOTS, 2):
            high, low = high_low(notes[row : row + 1, :] + notes[row + 1 : row + 2, :])
            notes[row : row + 1, :] = high
            notes[row + 1 : row + 2, :] = low
        out[...] = jnp.broadcast_to(notes[...].astype(out.dtype), out.shape)


def precondition(own, swapped):
    _, rows, part = own.shape
    order = RING * part
    kind = own.dtype
    return pl.pallas_call(
        block_kernel,
        out_shape=jax.ShapeDtypeStruct((COLS * RING, rows, part), kind),
        in_specs=[VMEM] * 2,
        out_specs=VMEM,
        scratch_shapes=[
            pltpu.VMEM((order, order), kind),
            pltpu.VMEM((order, order), kind),
            pltpu.VMEM((COLS, CORES, rows, order), kind),
            pltpu.VMEM((order, order), kind),
            pltpu.VMEM((COLS, CORES, rows, order), jnp.float32),
            pltpu.VMEM((rows, part), jnp.float32),
        ],
        compiler_params=limit(28),
        cost_estimate=pl.CostEstimate(flops=4 * order**3, bytes_accessed=10 * order * order, transcendentals=0),
        name="precondition",
    )(own, swapped)


def finish_kernel(place, returned, momentum, out, wide, adam):
    block_rows, shard_rows, block_cols, lanes = momentum.shape
    for col in range(COLS):
        note = jnp.sum(returned[member(col, NOTE)].astype(jnp.float32), axis=1, keepdims=True)
        adam[col * shard_rows : (col + 1) * shard_rows, :] = jnp.broadcast_to(note, (shard_rows, lanes))

    def step(i, carry):
        for j in range(block_cols):
            block = i * block_cols + j
            row = place[1, block]
            scale = jnp.sqrt(adam[pl.ds(row, 1), :] + adam[pl.ds(row + 1, 1), :])
            piece = returned[place[0, block]].astype(jnp.float32) * scale
            wide[pl.ds(j, shard_rows, stride=block_cols), :] = piece
        grafted = wide[...].reshape(shard_rows, block_cols, lanes)
        out[i] = (BETA_ONE * momentum[i].astype(jnp.float32) + grafted).astype(out.dtype)
        return carry

    lax.fori_loop(0, block_rows, step, 0)


def finish(place, returned, momentum):
    block_rows, shard_rows, block_cols, lanes = momentum.shape
    return pl.pallas_call(
        finish_kernel,
        out_shape=jax.ShapeDtypeStruct(momentum.shape, momentum.dtype),
        in_specs=[SMEM, VMEM, VMEM],
        out_specs=VMEM,
        scratch_shapes=[
            pltpu.VMEM((shard_rows * block_cols, lanes), jnp.float32),
            pltpu.VMEM((COLS * shard_rows, lanes), jnp.float32),
        ],
        compiler_params=limit(16),
        name="finish",
    )(place, returned, momentum)


def exchange(array):
    return lax.all_to_all(array, ("col", "replica"), split_axis=0, concat_axis=0, tiled=True)


def swap(array):
    return lax.ppermute(array, "core", [(0, 1), (1, 0)])


def local(gradient, second_moment, momentum, left_factor, right_factor, block_of_slot):
    moment_new, pieces, place, *spread = prepare(
        block_of_slot.T, gradient, second_moment, left_factor, right_factor
    )
    line = ("core", "replica")
    factors = [lax.ppermute(shard, line, factor_pairs(step)) for step, shard in enumerate(spread)]
    relayed = lax.ppermute(factors[0], line, relay_pairs())
    columns = lax.cond(lax.axis_index("core") < CORES, exchange, jnp.zeros_like, pieces)
    held = together(columns, [spread[0], relayed] + factors)
    parts = precondition(held, swap(held))
    return (finish(place, exchange(parts), momentum), moment_new)


def solution(mesh):
    fine = Mesh(mesh.devices.reshape(COLS, CORES, RING), ("col", "core", "replica"))
    fsdp = ("col", "core")
    in_specs = (
        P(None, fsdp, None, "replica"),
        P(None, fsdp, None, "replica"),
        P(None, fsdp, None, "replica"),
        P(fsdp, "replica", None),
        P(fsdp, None, "replica"),
        P(),
    )
    out_specs = (P(None, fsdp, None, "replica"), P(None, fsdp, None, "replica"))
    return jax.shard_map(local, mesh=fine, in_specs=in_specs, out_specs=out_specs, check_vma=False)
```

```python
import jax
import jax.numpy as jnp
from jax import lax
from jax.experimental import pallas as pl
from jax.experimental.pallas import tpu as pltpu
from jax.sharding import Mesh
from jax.sharding import PartitionSpec as P

BETA_ONE = 0.9
BETA_TWO = 0.999
ADAM_EPS = 1e-08
NORM_EPS = 1e-06

RING = 8
COLS = 32
SLOTS = 3
PLACES = 4
CORES = 2
NOTE = 3
CHUNKS = 4
RELAYED = (1, 0)
BESIDE = (-1, 1)
EARLY = 2

ANY = pl.BlockSpec(memory_space=pl.ANY)
HBM = pl.BlockSpec(memory_space=pltpu.HBM)
VMEM = pl.BlockSpec(memory_space=pltpu.VMEM)
SMEM = pl.BlockSpec(memory_space=pltpu.SMEM)


def limit(mebibytes):
    return pltpu.CompilerParams(vmem_limit_bytes=mebibytes * 1024 * 1024)


def high_low(value):
    high = value.astype(jnp.bfloat16).astype(jnp.float32)
    return high, value - high


def member(col, place):
    return col * RING + place


def factor_pairs(step):
    pairs = []
    for c in range(CORES):
        for s in range(SLOTS):
            root = PLACES * c + s
            near, far = (root + step) % RING, (root + step + PLACES) % RING
            if step > 0:
                pairs.append((c * RING + near, c * RING + root))
                pairs.append((c * RING + far, (1 - c) * RING + root))
            elif s == RELAYED[c]:
                pairs.append((c * RING + far, c * RING + (root + BESIDE[c]) % RING))
            else:
                pairs.append((c * RING + far, (1 - c) * RING + root))
    return pairs


def relay_pairs():
    pairs = []
    for c in range(CORES):
        root = PLACES * c + RELAYED[c]
        pairs.append((c * RING + (root + BESIDE[c]) % RING, (1 - c) * RING + root))
    return pairs


def factor_kernel(left, right, *refs):
    outs, held_left, held_right, spread, sems = refs[:PLACES], *refs[PLACES:]
    part = left.shape[1]
    here = lax.axis_index("replica")
    copies = []
    for s in range(SLOTS):
        copies.append(pltpu.make_async_copy(left.at[s], held_left.at[s], sems.at[0, s]))
        copies.append(pltpu.make_async_copy(right.at[s], held_right.at[s], sems.at[1, s]))
    for copy in copies:
        copy.start()
    for copy in copies:
        copy.wait()
    out_copies = [pltpu.make_async_copy(spread.at[step], outs[step], sems.at[2, step]) for step in range(PLACES)]
    for step in range(PLACES):
        slot = lax.rem(here - step + RING, PLACES)

        @pl.when(slot < SLOTS)
        def _():
            for j in range(RING):
                spread[step, j] = held_left[slot, :, j * part : (j + 1) * part]
                spread[step, RING + j] = held_right[slot, j * part : (j + 1) * part, :]
            out_copies[step].start()

    for step in range(PLACES):
        slot = lax.rem(here - step + RING, PLACES)

        @pl.when(slot < SLOTS)
        def _():
            out_copies[step].wait()


def spread_factors(left, right):
    part = left.shape[1]
    shape = (2 * RING, part, part)
    return pl.pallas_call(
        factor_kernel,
        out_shape=[jax.ShapeDtypeStruct(shape, left.dtype)] * PLACES,
        in_specs=[HBM, HBM],
        out_specs=[HBM] * PLACES,
        scratch_shapes=[
            pltpu.VMEM(left.shape, left.dtype),
            pltpu.VMEM(right.shape, right.dtype),
            pltpu.VMEM((PLACES,) + shape, left.dtype),
            pltpu.SemaphoreType.DMA((3, PLACES)),
        ],
        compiler_params=limit(63),
        name="spread_factors",
    )(left, right)


def prepare_kernel(slots, gradient, second, after, moment, pieces, place, *scratch):
    held_gradient, held_second, held_moment, wide, square, notes, sems = scratch
    block_rows, shard_rows, block_cols, lanes = gradient.shape
    per_row = shard_rows * block_cols
    chunk = block_rows // CHUNKS
    chunks = [pl.ds(at * chunk, chunk) for at in range(CHUNKS)]
    first, second_in, out = [], [], []
    for at, rows in enumerate(chunks):
        first.append(pltpu.make_async_copy(gradient.at[rows], held_gradient.at[rows], sems.at[0, at]))
        second_in.append(pltpu.make_async_copy(second.at[rows], held_second.at[rows], sems.at[1, at]))
        out.append(pltpu.make_async_copy(held_moment.at[rows], moment.at[rows], sems.at[2, at]))
        first[at].start()
        second_in[at].start()

    def adam(i, carry):
        g = held_gradient[i].astype(jnp.float32)
        v = BETA_TWO * held_second[i].astype(jnp.float32) + (1.0 - BETA_TWO) * g * g
        held_moment[i] = v.astype(moment.dtype)
        step = g / (jnp.sqrt(v) + ADAM_EPS)
        square[pl.ds(pl.multiple_of(i * block_cols, block_cols), block_cols), :] = jnp.sum(step * step, axis=0)
        wide[pl.ds(pl.multiple_of(i * per_row, per_row), per_row), :] = g.reshape(per_row, lanes)
        return carry

    for at in range(CHUNKS):
        first[at].wait()
        second_in[at].wait()
        lax.fori_loop(at * chunk, (at + 1) * chunk, adam, 0)
        out[at].start()
    notes[...] = jnp.zeros(notes.shape, notes.dtype)

    def column(col, carry):
        for c in range(CORES):
            for s in range(SLOTS):
                held = slots[s, col * CORES + c]
                block = jnp.maximum(held, 0)
                i = lax.div(block, block_cols)
                j = lax.rem(block, block_cols)
                piece = wide[pl.ds(i * per_row + j, shard_rows, stride=block_cols), :]
                pieces[member(col, PLACES * c + s)] = piece.astype(pieces.dtype)
                high, low = high_low(square[pl.ds(block, 1), :])
                row = 2 * (SLOTS * c + s)
                notes[row : row + 1, :] = high
                notes[row + 1 : row + 2, :] = low

                @pl.when(held >= 0)
                def _():
                    place[0, block] = member(col, PLACES * c + s)
                    place[1, block] = col * shard_rows + row

        pieces[member(col, NOTE)] = notes[...].astype(pieces.dtype)
        return carry

    lax.fori_loop(0, COLS, column, 0)
    for copy in out:
        copy.wait()


def prepare(slots, gradient, second, after):
    block_rows, shard_rows, block_cols, lanes = gradient.shape
    block_count = block_rows * block_cols
    return pl.pallas_call(
        prepare_kernel,
        out_shape=[
            jax.ShapeDtypeStruct(second.shape, second.dtype),
            jax.ShapeDtypeStruct((COLS * RING, shard_rows, lanes), gradient.dtype),
            jax.ShapeDtypeStruct((2, block_count), jnp.int32),
        ],
        in_specs=[SMEM, HBM, HBM, ANY],
        out_specs=[HBM, VMEM, SMEM],
        scratch_shapes=[
            pltpu.VMEM(gradient.shape, gradient.dtype),
            pltpu.VMEM(second.shape, second.dtype),
            pltpu.VMEM(second.shape, second.dtype),
            pltpu.VMEM((block_count * shard_rows, lanes), jnp.float32),
            pltpu.VMEM((block_count, lanes), jnp.float32),
            pltpu.VMEM((shard_rows, lanes), jnp.float32),
            pltpu.SemaphoreType.DMA((3, CHUNKS)),
        ],
        compiler_params=limit(63),
        name="prepare",
    )(slots, gradient, second, after)


def released_kernel(*refs):
    pass


def released(arrays, other):
    count = len(arrays)
    return pl.pallas_call(
        released_kernel,
        out_shape=[jax.ShapeDtypeStruct(array.shape, array.dtype) for array in arrays],
        in_specs=[ANY] * (count + 1),
        out_specs=[ANY] * count,
        input_output_aliases={at: at for at in range(count)},
        compiler_params=limit(63),
        name="released",
    )(*arrays, other)


def together_kernel(columns, own, relayed, *refs):
    factors, out = refs[:PLACES], refs[PLACES]
    count, rows, part = columns.shape
    size = own.shape[0] * own.shape[1] // rows
    here = lax.axis_index("replica")
    at_home = lax.div(here, PLACES) == lax.axis_index("core")
    slot = lax.rem(here, PLACES)
    direct = slot != jnp.where(here < PLACES, RELAYED[0], RELAYED[1])
    out[:count] = columns[...]
    for step in range(1, PLACES):
        out[count + step * size : count + (step + 1) * size] = factors[step][...].reshape(size, rows, part)

    @pl.when(at_home)
    def _():
        out[count : count + size] = own[...].reshape(size, rows, part)

    @pl.when(jnp.logical_not(at_home) & direct)
    def _():
        out[count : count + size] = factors[0][...].reshape(size, rows, part)

    @pl.when(jnp.logical_not(at_home) & jnp.logical_not(direct))
    def _():
        out[count : count + size] = relayed[...].reshape(size, rows, part)


def together(columns, shards):
    count, rows, part = columns.shape
    count += PLACES * shards[0].shape[0] * shards[0].shape[1] // rows
    return pl.pallas_call(
        together_kernel,
        out_shape=jax.ShapeDtypeStruct((count, rows, part), columns.dtype),
        in_specs=[VMEM] * (1 + len(shards)),
        out_specs=VMEM,
        compiler_params=limit(16),
        name="together",
    )(columns, *shards)


def block_kernel(own, swapped, out, lf, rf, grad, half, full, notes):
    rows, part = own.shape[1:]
    order = lf.shape[0]
    count = COLS * RING
    groups = part // rows
    core = lax.axis_index("core")
    here = lax.axis_index("replica")
    place = lax.rem(here, PLACES)

    @pl.when(place < SLOTS)
    def _():
        owner_core = lax.div(here, PLACES)
        for b, held in enumerate((own, swapped)):
            h = core if b == 0 else 1 - core
            for col in range(COLS):
                for r in range(RING):
                    grad[col, h, :, r * part : (r + 1) * part] = held[member(col, r)]
            for step in range(PLACES):
                source = lax.rem(here + step + jnp.where(h == owner_core, 0, PLACES), RING)
                at = pl.ds(pl.multiple_of(source * part, part), part)
                for j in range(RING):
                    left = count + (2 * RING * step + j) * groups
                    right = left + RING * groups
                    lf[at, j * part : (j + 1) * part] = held[left : left + groups].reshape(part, part)
                    rf[j * part : (j + 1) * part, at] = held[right : right + groups].reshape(part, part)

        tile = 2 * part
        steps = order // tile

        def first(t, carry):
            at = pl.ds(pl.multiple_of(t * tile, tile), tile)
            rhs = grad[:, :, :, at].reshape(order, tile)
            half[:, at] = jnp.dot(lf[...], rhs, preferred_element_type=jnp.float32).astype(half.dtype)
            return carry

        lax.fori_loop(0, steps, first, 0, unroll=True)

        def second(t, square):
            at = pl.ds(pl.multiple_of(t * tile, tile), tile)
            value = jnp.dot(half[...], rf[:, at], preferred_element_type=jnp.float32)
            full[:, :, :, at] = value.reshape(COLS, CORES, rows, tile)
            return square + jnp.sum(value * value, axis=0, keepdims=True)

        square = lax.fori_loop(0, steps, second, jnp.zeros((1, tile), jnp.float32), unroll=True)
        square = jnp.sum(square, axis=1, keepdims=True)
        scale = 1.0 / jnp.sqrt(square + NORM_EPS)
        for r in range(RING):
            value = (full[:, core, :, r * part : (r + 1) * part] * scale).astype(out.dtype)
            for col in range(COLS):
                out[member(col, r)] = value[col]

    @pl.when(place == NOTE)
    def _():
        total = jnp.zeros(notes.shape, jnp.float32)
        for held in (own, swapped):
            total = total + jnp.sum(held[:count].astype(jnp.float32), axis=0)
        notes[...] = total
        for row in range(0, 2 * CORES * SLOTS, 2):
            high, low = high_low(notes[row : row + 1, :] + notes[row + 1 : row + 2, :])
            notes[row : row + 1, :] = high
            notes[row + 1 : row + 2, :] = low
        out[...] = jnp.broadcast_to(notes[...].astype(out.dtype), out.shape)


def precondition(own, swapped):
    _, rows, part = own.shape
    order = RING * part
    kind = own.dtype
    return pl.pallas_call(
        block_kernel,
        out_shape=jax.ShapeDtypeStruct((COLS * RING, rows, part), kind),
        in_specs=[VMEM] * 2,
        out_specs=VMEM,
        scratch_shapes=[
            pltpu.VMEM((order, order), kind),
            pltpu.VMEM((order, order), kind),
            pltpu.VMEM((COLS, CORES, rows, order), kind),
            pltpu.VMEM((order, order), kind),
            pltpu.VMEM((COLS, CORES, rows, order), jnp.float32),
            pltpu.VMEM((rows, part), jnp.float32),
        ],
        compiler_params=limit(28),
        cost_estimate=pl.CostEstimate(flops=4 * order**3, bytes_accessed=10 * order * order, transcendentals=0),
        name="precondition",
    )(own, swapped)


def finish_kernel(place, returned, momentum, out, wide, adam):
    block_rows, shard_rows, block_cols, lanes = momentum.shape
    for col in range(COLS):
        note = jnp.sum(returned[member(col, NOTE)].astype(jnp.float32), axis=1, keepdims=True)
        adam[col * shard_rows : (col + 1) * shard_rows, :] = jnp.broadcast_to(note, (shard_rows, lanes))

    def step(i, carry):
        for j in range(block_cols):
            block = i * block_cols + j
            row = place[1, block]
            scale = jnp.sqrt(adam[pl.ds(row, 1), :] + adam[pl.ds(row + 1, 1), :])
            piece = returned[place[0, block]].astype(jnp.float32) * scale
            wide[pl.ds(j, shard_rows, stride=block_cols), :] = piece
        grafted = wide[...].reshape(shard_rows, block_cols, lanes)
        out[i] = (BETA_ONE * momentum[i].astype(jnp.float32) + grafted).astype(out.dtype)
        return carry

    lax.fori_loop(0, block_rows, step, 0, unroll=2)


def finish(place, returned, momentum):
    block_rows, shard_rows, block_cols, lanes = momentum.shape
    return pl.pallas_call(
        finish_kernel,
        out_shape=jax.ShapeDtypeStruct(momentum.shape, momentum.dtype),
        in_specs=[SMEM, VMEM, VMEM],
        out_specs=VMEM,
        scratch_shapes=[
            pltpu.VMEM((shard_rows * block_cols, lanes), jnp.float32),
            pltpu.VMEM((COLS * shard_rows, lanes), jnp.float32),
        ],
        compiler_params=limit(16),
        name="finish",
    )(place, returned, momentum)


def exchange(array):
    return lax.all_to_all(array, ("col", "replica"), split_axis=0, concat_axis=0, tiled=True)


def swap(array):
    return lax.ppermute(array, "core", [(0, 1), (1, 0)])


def local(gradient, second_moment, momentum, left_factor, right_factor, block_of_slot):
    spread = spread_factors(left_factor, right_factor)
    line = ("core", "replica")
    factors = [lax.ppermute(spread[step], line, factor_pairs(step)) for step in range(EARLY)]
    moment_new, pieces, place = prepare(block_of_slot.T, gradient, second_moment, spread[0])
    later = released(spread[EARLY:], pieces)
    factors += [lax.ppermute(shard, line, factor_pairs(EARLY + at)) for at, shard in enumerate(later)]
    factors[:1] = released(factors[:1], pieces)
    relayed = lax.ppermute(factors[0], line, relay_pairs())
    columns = lax.cond(lax.axis_index("core") < CORES, exchange, jnp.zeros_like, pieces)
    held = together(columns, [spread[0], relayed] + factors)
    parts = precondition(held, swap(held))
    return (finish(place, exchange(parts), momentum), moment_new)


def solution(mesh):
    fine = Mesh(mesh.devices.reshape(COLS, CORES, RING), ("col", "core", "replica"))
    fsdp = ("col", "core")
    in_specs = (
        P(None, fsdp, None, "replica"),
        P(None, fsdp, None, "replica"),
        P(None, fsdp, None, "replica"),
        P(fsdp, "replica", None),
        P(fsdp, None, "replica"),
        P(),
    )
    out_specs = (P(None, fsdp, None, "replica"), P(None, fsdp, None, "replica"))
    return jax.shard_map(local, mesh=fine, in_specs=in_specs, out_specs=out_specs, check_vma=False)
```

```python
import jax
import jax.numpy as jnp
from jax import lax
from jax.experimental import pallas as pl
from jax.experimental.pallas import tpu as pltpu
from jax.sharding import Mesh
from jax.sharding import PartitionSpec as P

BETA_ONE = 0.9
BETA_TWO = 0.999
ADAM_EPS = 1e-08
NORM_EPS = 1e-06

RING = 8
COLS = 32
SLOTS = 3
PLACES = 4
CORES = 2
NOTE = 3
CHUNKS = 4
TURN = 2
EARLY = 2

ANY = pl.BlockSpec(memory_space=pl.ANY)
HBM = pl.BlockSpec(memory_space=pltpu.HBM)
VMEM = pl.BlockSpec(memory_space=pltpu.VMEM)
SMEM = pl.BlockSpec(memory_space=pltpu.SMEM)


def limit(mebibytes):
    return pltpu.CompilerParams(vmem_limit_bytes=mebibytes * 1024 * 1024)


def high_low(value):
    high = value.astype(jnp.bfloat16).astype(jnp.float32)
    return high, value - high


def member(col, place):
    return col * RING + place


def chip_of(place):
    return (place + TURN) % RING


def place_here():
    return lax.rem(lax.axis_index("replica") + RING - TURN, RING)


def factor_pairs(step):
    pairs = []
    for c in range(CORES):
        for s in range(SLOTS):
            root = chip_of(PLACES * c + s)
            near, far = (root + step) % RING, (root + step + PLACES) % RING
            if step > 0:
                pairs.append((c * RING + near, c * RING + root))
            pairs.append((c * RING + far, (1 - c) * RING + root))
    return pairs


def factor_kernel(left, right, *refs):
    outs, held_left, held_right, spread, sems = refs[:PLACES], *refs[PLACES:]
    part = left.shape[1]
    here = place_here()
    copies = []
    for s in range(SLOTS):
        copies.append(pltpu.make_async_copy(left.at[s], held_left.at[s], sems.at[0, s]))
        copies.append(pltpu.make_async_copy(right.at[s], held_right.at[s], sems.at[1, s]))
    for copy in copies:
        copy.start()
    for copy in copies:
        copy.wait()
    out_copies = [pltpu.make_async_copy(spread.at[step], outs[step], sems.at[2, step]) for step in range(PLACES)]
    for step in range(PLACES):
        slot = lax.rem(here - step + RING, PLACES)

        @pl.when(slot < SLOTS)
        def _():
            for j in range(RING):
                spread[step, j] = held_left[slot, :, j * part : (j + 1) * part]
                spread[step, RING + j] = held_right[slot, j * part : (j + 1) * part, :]
            out_copies[step].start()

    for step in range(PLACES):
        slot = lax.rem(here - step + RING, PLACES)

        @pl.when(slot < SLOTS)
        def _():
            out_copies[step].wait()


def spread_factors(left, right):
    part = left.shape[1]
    shape = (2 * RING, part, part)
    return pl.pallas_call(
        factor_kernel,
        out_shape=[jax.ShapeDtypeStruct(shape, left.dtype)] * PLACES,
        in_specs=[HBM, HBM],
        out_specs=[HBM] * PLACES,
        scratch_shapes=[
            pltpu.VMEM(left.shape, left.dtype),
            pltpu.VMEM(right.shape, right.dtype),
            pltpu.VMEM((PLACES,) + shape, left.dtype),
            pltpu.SemaphoreType.DMA((3, PLACES)),
        ],
        compiler_params=limit(63),
        name="spread_factors",
    )(left, right)


def prepare_kernel(slots, gradient, second, after, moment, pieces, place, *scratch):
    held_gradient, held_second, held_moment, wide, square, notes, sems = scratch
    block_rows, shard_rows, block_cols, lanes = gradient.shape
    per_row = shard_rows * block_cols
    chunk = block_rows // CHUNKS
    chunks = [pl.ds(at * chunk, chunk) for at in range(CHUNKS)]
    first, second_in, out = [], [], []
    for at, rows in enumerate(chunks):
        first.append(pltpu.make_async_copy(gradient.at[rows], held_gradient.at[rows], sems.at[0, at]))
        second_in.append(pltpu.make_async_copy(second.at[rows], held_second.at[rows], sems.at[1, at]))
        out.append(pltpu.make_async_copy(held_moment.at[rows], moment.at[rows], sems.at[2, at]))
        first[at].start()
        second_in[at].start()

    def adam(i, carry):
        g = held_gradient[i].astype(jnp.float32)
        v = BETA_TWO * held_second[i].astype(jnp.float32) + (1.0 - BETA_TWO) * g * g
        held_moment[i] = v.astype(moment.dtype)
        step = g / (jnp.sqrt(v) + ADAM_EPS)
        square[pl.ds(pl.multiple_of(i * block_cols, block_cols), block_cols), :] = jnp.sum(step * step, axis=0)
        wide[pl.ds(pl.multiple_of(i * per_row, per_row), per_row), :] = g.reshape(per_row, lanes)
        return carry

    for at in range(CHUNKS):
        first[at].wait()
        second_in[at].wait()
        lax.fori_loop(at * chunk, (at + 1) * chunk, adam, 0)
        out[at].start()
    notes[...] = jnp.zeros(notes.shape, notes.dtype)

    def column(col, carry):
        for c in range(CORES):
            for s in range(SLOTS):
                held = slots[s, col * CORES + c]
                block = jnp.maximum(held, 0)
                i = lax.div(block, block_cols)
                j = lax.rem(block, block_cols)
                piece = wide[pl.ds(i * per_row + j, shard_rows, stride=block_cols), :]
                pieces[member(col, chip_of(PLACES * c + s))] = piece.astype(pieces.dtype)
                high, low = high_low(square[pl.ds(block, 1), :])
                row = 2 * (SLOTS * c + s)
                notes[row : row + 1, :] = high
                notes[row + 1 : row + 2, :] = low

                @pl.when(held >= 0)
                def _():
                    place[0, block] = member(col, chip_of(PLACES * c + s))
                    place[1, block] = col * shard_rows + row

        pieces[member(col, chip_of(NOTE))] = notes[...].astype(pieces.dtype)
        return carry

    lax.fori_loop(0, COLS, column, 0)
    for copy in out:
        copy.wait()


def prepare(slots, gradient, second, after):
    block_rows, shard_rows, block_cols, lanes = gradient.shape
    block_count = block_rows * block_cols
    return pl.pallas_call(
        prepare_kernel,
        out_shape=[
            jax.ShapeDtypeStruct(second.shape, second.dtype),
            jax.ShapeDtypeStruct((COLS * RING, shard_rows, lanes), gradient.dtype),
            jax.ShapeDtypeStruct((2, block_count), jnp.int32),
        ],
        in_specs=[SMEM, HBM, HBM, ANY],
        out_specs=[HBM, VMEM, SMEM],
        scratch_shapes=[
            pltpu.VMEM(gradient.shape, gradient.dtype),
            pltpu.VMEM(second.shape, second.dtype),
            pltpu.VMEM(second.shape, second.dtype),
            pltpu.VMEM((block_count * shard_rows, lanes), jnp.float32),
            pltpu.VMEM((block_count, lanes), jnp.float32),
            pltpu.VMEM((shard_rows, lanes), jnp.float32),
            pltpu.SemaphoreType.DMA((3, CHUNKS)),
        ],
        compiler_params=limit(63),
        name="prepare",
    )(slots, gradient, second, after)


def released_kernel(*refs):
    pass


def released(arrays, other):
    count = len(arrays)
    return pl.pallas_call(
        released_kernel,
        out_shape=[jax.ShapeDtypeStruct(array.shape, array.dtype) for array in arrays],
        in_specs=[ANY] * (count + 1),
        out_specs=[ANY] * count,
        input_output_aliases={at: at for at in range(count)},
        compiler_params=limit(63),
        name="released",
    )(*arrays, other)


def together_kernel(columns, own, *refs):
    factors, out = refs[:PLACES], refs[PLACES]
    count, rows, part = columns.shape
    size = own.shape[0] * own.shape[1] // rows
    at_home = lax.div(place_here(), PLACES) == lax.axis_index("core")
    out[:count] = columns[...]
    for step in range(1, PLACES):
        out[count + step * size : count + (step + 1) * size] = factors[step][...].reshape(size, rows, part)

    @pl.when(at_home)
    def _():
        out[count : count + size] = own[...].reshape(size, rows, part)

    @pl.when(jnp.logical_not(at_home))
    def _():
        out[count : count + size] = factors[0][...].reshape(size, rows, part)


def together(columns, shards):
    count, rows, part = columns.shape
    count += PLACES * shards[0].shape[0] * shards[0].shape[1] // rows
    return pl.pallas_call(
        together_kernel,
        out_shape=jax.ShapeDtypeStruct((count, rows, part), columns.dtype),
        in_specs=[VMEM] * (1 + len(shards)),
        out_specs=VMEM,
        compiler_params=limit(16),
        name="together",
    )(columns, *shards)


def block_kernel(own, swapped, out, lf, rf, grad, half, full, notes):
    rows, part = own.shape[1:]
    order = lf.shape[0]
    count = COLS * RING
    groups = part // rows
    core = lax.axis_index("core")
    here = lax.axis_index("replica")
    place = lax.rem(place_here(), PLACES)

    @pl.when(place < SLOTS)
    def _():
        owner_core = lax.div(place_here(), PLACES)
        for b, held in enumerate((own, swapped)):
            h = core if b == 0 else 1 - core
            for col in range(COLS):
                for r in range(RING):
                    grad[col, h, :, r * part : (r + 1) * part] = held[member(col, r)]
            for step in range(PLACES):
                source = lax.rem(here + step + jnp.where(h == owner_core, 0, PLACES), RING)
                at = pl.ds(pl.multiple_of(source * part, part), part)
                for j in range(RING):
                    left = count + (2 * RING * step + j) * groups
                    right = left + RING * groups
                    lf[at, j * part : (j + 1) * part] = held[left : left + groups].reshape(part, part)
                    rf[j * part : (j + 1) * part, at] = held[right : right + groups].reshape(part, part)

        tile = 2 * part
        steps = order // tile

        def first(t, carry):
            at = pl.ds(pl.multiple_of(t * tile, tile), tile)
            rhs = grad[:, :, :, at].reshape(order, tile)
            half[:, at] = jnp.dot(lf[...], rhs, preferred_element_type=jnp.float32).astype(half.dtype)
            return carry

        lax.fori_loop(0, steps, first, 0, unroll=True)

        def second(t, square):
            at = pl.ds(pl.multiple_of(t * tile, tile), tile)
            value = jnp.dot(half[...], rf[:, at], preferred_element_type=jnp.float32)
            full[:, :, :, at] = value.reshape(COLS, CORES, rows, tile)
            return square + jnp.sum(value * value, axis=0, keepdims=True)

        square = lax.fori_loop(0, steps, second, jnp.zeros((1, tile), jnp.float32), unroll=True)
        square = jnp.sum(square, axis=1, keepdims=True)
        scale = 1.0 / jnp.sqrt(square + NORM_EPS)
        for r in range(RING):
            value = (full[:, core, :, r * part : (r + 1) * part] * scale).astype(out.dtype)
            for col in range(COLS):
                out[member(col, r)] = value[col]

    @pl.when(place == NOTE)
    def _():
        total = jnp.zeros(notes.shape, jnp.float32)
        for held in (own, swapped):
            total = total + jnp.sum(held[:count].astype(jnp.float32), axis=0)
        notes[...] = total
        for row in range(0, 2 * CORES * SLOTS, 2):
            high, low = high_low(notes[row : row + 1, :] + notes[row + 1 : row + 2, :])
            notes[row : row + 1, :] = high
            notes[row + 1 : row + 2, :] = low
        out[...] = jnp.broadcast_to(notes[...].astype(out.dtype), out.shape)


def precondition(own, swapped):
    _, rows, part = own.shape
    order = RING * part
    kind = own.dtype
    return pl.pallas_call(
        block_kernel,
        out_shape=jax.ShapeDtypeStruct((COLS * RING, rows, part), kind),
        in_specs=[VMEM] * 2,
        out_specs=VMEM,
        scratch_shapes=[
            pltpu.VMEM((order, order), kind),
            pltpu.VMEM((order, order), kind),
            pltpu.VMEM((COLS, CORES, rows, order), kind),
            pltpu.VMEM((order, order), kind),
            pltpu.VMEM((COLS, CORES, rows, order), jnp.float32),
            pltpu.VMEM((rows, part), jnp.float32),
        ],
        compiler_params=limit(28),
        cost_estimate=pl.CostEstimate(flops=4 * order**3, bytes_accessed=10 * order * order, transcendentals=0),
        name="precondition",
    )(own, swapped)


def finish_kernel(place, returned, momentum, out, wide, adam):
    block_rows, shard_rows, block_cols, lanes = momentum.shape
    for col in range(COLS):
        note = jnp.sum(returned[member(col, chip_of(NOTE))].astype(jnp.float32), axis=1, keepdims=True)
        adam[col * shard_rows : (col + 1) * shard_rows, :] = jnp.broadcast_to(note, (shard_rows, lanes))

    def step(i, carry):
        for j in range(block_cols):
            block = i * block_cols + j
            row = place[1, block]
            scale = jnp.sqrt(adam[pl.ds(row, 1), :] + adam[pl.ds(row + 1, 1), :])
            piece = returned[place[0, block]].astype(jnp.float32) * scale
            wide[pl.ds(j, shard_rows, stride=block_cols), :] = piece
        grafted = wide[...].reshape(shard_rows, block_cols, lanes)
        out[i] = (BETA_ONE * momentum[i].astype(jnp.float32) + grafted).astype(out.dtype)
        return carry

    lax.fori_loop(0, block_rows, step, 0, unroll=2)


def finish(place, returned, momentum):
    block_rows, shard_rows, block_cols, lanes = momentum.shape
    return pl.pallas_call(
        finish_kernel,
        out_shape=jax.ShapeDtypeStruct(momentum.shape, momentum.dtype),
        in_specs=[SMEM, VMEM, VMEM],
        out_specs=VMEM,
        scratch_shapes=[
            pltpu.VMEM((shard_rows * block_cols, lanes), jnp.float32),
            pltpu.VMEM((COLS * shard_rows, lanes), jnp.float32),
        ],
        compiler_params=limit(16),
        name="finish",
    )(place, returned, momentum)


def exchange(array):
    return lax.all_to_all(array, ("col", "replica"), split_axis=0, concat_axis=0, tiled=True)


def swap(array):
    return lax.ppermute(array, "core", [(0, 1), (1, 0)])


def local(gradient, second_moment, momentum, left_factor, right_factor, block_of_slot):
    spread = spread_factors(left_factor, right_factor)
    line = ("core", "replica")
    factors = [lax.ppermute(spread[step], line, factor_pairs(step)) for step in range(EARLY)]
    moment_new, pieces, place = prepare(block_of_slot.T, gradient, second_moment, spread[0])
    later = released(spread[EARLY:], pieces)
    factors += [lax.ppermute(shard, line, factor_pairs(EARLY + at)) for at, shard in enumerate(later)]
    columns = lax.cond(lax.axis_index("core") < CORES, exchange, jnp.zeros_like, pieces)
    held = together(columns, [spread[0]] + factors)
    parts = precondition(held, swap(held))
    return (finish(place, exchange(parts), momentum), moment_new)


def solution(mesh):
    fine = Mesh(mesh.devices.reshape(COLS, CORES, RING), ("col", "core", "replica"))
    fsdp = ("col", "core")
    in_specs = (
        P(None, fsdp, None, "replica"),
        P(None, fsdp, None, "replica"),
        P(None, fsdp, None, "replica"),
        P(fsdp, "replica", None),
        P(fsdp, None, "replica"),
        P(),
    )
    out_specs = (P(None, fsdp, None, "replica"), P(None, fsdp, None, "replica"))
    return jax.shard_map(local, mesh=fine, in_specs=in_specs, out_specs=out_specs, check_vma=False)
```

```python
import jax
import jax.numpy as jnp
from jax import lax
from jax.experimental import pallas as pl
from jax.experimental.pallas import tpu as pltpu
from jax.sharding import Mesh
from jax.sharding import PartitionSpec as P

BETA_ONE = 0.9
BETA_TWO = 0.999
ADAM_EPS = 1e-08
NORM_EPS = 1e-06

RING = 8
COLS = 32
SLOTS = 3
PLACES = 4
CORES = 2
NOTE = 3
CHUNKS = 4
TURN = 2
EARLY = 3

ANY = pl.BlockSpec(memory_space=pl.ANY)
HBM = pl.BlockSpec(memory_space=pltpu.HBM)
VMEM = pl.BlockSpec(memory_space=pltpu.VMEM)
SMEM = pl.BlockSpec(memory_space=pltpu.SMEM)


def limit(mebibytes):
    return pltpu.CompilerParams(vmem_limit_bytes=mebibytes * 1024 * 1024)


def high_low(value):
    high = value.astype(jnp.bfloat16).astype(jnp.float32)
    return high, value - high


def member(col, place):
    return col * RING + place


def chip_of(place):
    return (place + TURN) % RING


def place_here():
    return lax.rem(lax.axis_index("replica") + RING - TURN, RING)


def factor_pairs(step):
    pairs = []
    for c in range(CORES):
        for s in range(SLOTS):
            root = chip_of(PLACES * c + s)
            near, far = (root + step) % RING, (root + step + PLACES) % RING
            if step > 0:
                pairs.append((c * RING + near, c * RING + root))
            pairs.append((c * RING + far, (1 - c) * RING + root))
    return pairs


def factor_kernel(left, right, *refs):
    outs, held_left, held_right, spread, sems = refs[:PLACES], *refs[PLACES:]
    part = left.shape[1]
    here = place_here()
    copies = []
    for s in range(SLOTS):
        copies.append(pltpu.make_async_copy(left.at[s], held_left.at[s], sems.at[0, s]))
        copies.append(pltpu.make_async_copy(right.at[s], held_right.at[s], sems.at[1, s]))
    for copy in copies:
        copy.start()
    for copy in copies:
        copy.wait()
    out_copies = [pltpu.make_async_copy(spread.at[step], outs[step], sems.at[2, step]) for step in range(PLACES)]
    for step in range(PLACES):
        slot = lax.rem(here - step + RING, PLACES)

        @pl.when(slot < SLOTS)
        def _():
            for j in range(RING):
                spread[step, j] = held_left[slot, :, j * part : (j + 1) * part]
                spread[step, RING + j] = held_right[slot, j * part : (j + 1) * part, :]
            out_copies[step].start()

    for step in range(PLACES):
        slot = lax.rem(here - step + RING, PLACES)

        @pl.when(slot < SLOTS)
        def _():
            out_copies[step].wait()


def spread_factors(left, right):
    part = left.shape[1]
    shape = (2 * RING, part, part)
    return pl.pallas_call(
        factor_kernel,
        out_shape=[jax.ShapeDtypeStruct(shape, left.dtype)] * PLACES,
        in_specs=[HBM, HBM],
        out_specs=[HBM] * PLACES,
        scratch_shapes=[
            pltpu.VMEM(left.shape, left.dtype),
            pltpu.VMEM(right.shape, right.dtype),
            pltpu.VMEM((PLACES,) + shape, left.dtype),
            pltpu.SemaphoreType.DMA((3, PLACES)),
        ],
        compiler_params=limit(63),
        name="spread_factors",
    )(left, right)


def prepare_kernel(slots, gradient, second, after, moment, pieces, place, *scratch):
    held_gradient, held_second, held_moment, wide, square, notes, sems = scratch
    block_rows, shard_rows, block_cols, lanes = gradient.shape
    per_row = shard_rows * block_cols
    chunk = block_rows // CHUNKS
    chunks = [pl.ds(at * chunk, chunk) for at in range(CHUNKS)]
    first, second_in, out = [], [], []
    for at, rows in enumerate(chunks):
        first.append(pltpu.make_async_copy(gradient.at[rows], held_gradient.at[rows], sems.at[0, at]))
        second_in.append(pltpu.make_async_copy(second.at[rows], held_second.at[rows], sems.at[1, at]))
        out.append(pltpu.make_async_copy(held_moment.at[rows], moment.at[rows], sems.at[2, at]))
        first[at].start()
        second_in[at].start()

    def adam(i, carry):
        g = held_gradient[i].astype(jnp.float32)
        v = BETA_TWO * held_second[i].astype(jnp.float32) + (1.0 - BETA_TWO) * g * g
        held_moment[i] = v.astype(moment.dtype)
        step = g / (jnp.sqrt(v) + ADAM_EPS)
        square[pl.ds(pl.multiple_of(i * block_cols, block_cols), block_cols), :] = jnp.sum(step * step, axis=0)
        wide[pl.ds(pl.multiple_of(i * per_row, per_row), per_row), :] = g.reshape(per_row, lanes)
        return carry

    for at in range(CHUNKS):
        first[at].wait()
        second_in[at].wait()
        lax.fori_loop(at * chunk, (at + 1) * chunk, adam, 0)
        out[at].start()
    notes[...] = jnp.zeros(notes.shape, notes.dtype)

    def column(col, carry):
        for c in range(CORES):
            for s in range(SLOTS):
                held = slots[s, col * CORES + c]
                block = jnp.maximum(held, 0)
                i = lax.div(block, block_cols)
                j = lax.rem(block, block_cols)
                piece = wide[pl.ds(i * per_row + j, shard_rows, stride=block_cols), :]
                pieces[member(col, chip_of(PLACES * c + s))] = piece.astype(pieces.dtype)
                high, low = high_low(square[pl.ds(block, 1), :])
                row = 2 * (SLOTS * c + s)
                notes[row : row + 1, :] = high
                notes[row + 1 : row + 2, :] = low

                @pl.when(held >= 0)
                def _():
                    place[0, block] = member(col, chip_of(PLACES * c + s))
                    place[1, block] = col * shard_rows + row

        pieces[member(col, chip_of(NOTE))] = notes[...].astype(pieces.dtype)
        return carry

    lax.fori_loop(0, COLS, column, 0)
    for copy in out:
        copy.wait()


def prepare(slots, gradient, second, after):
    block_rows, shard_rows, block_cols, lanes = gradient.shape
    block_count = block_rows * block_cols
    return pl.pallas_call(
        prepare_kernel,
        out_shape=[
            jax.ShapeDtypeStruct(second.shape, second.dtype),
            jax.ShapeDtypeStruct((COLS * RING, shard_rows, lanes), gradient.dtype),
            jax.ShapeDtypeStruct((2, block_count), jnp.int32),
        ],
        in_specs=[SMEM, HBM, HBM, ANY],
        out_specs=[HBM, VMEM, SMEM],
        scratch_shapes=[
            pltpu.VMEM(gradient.shape, gradient.dtype),
            pltpu.VMEM(second.shape, second.dtype),
            pltpu.VMEM(second.shape, second.dtype),
            pltpu.VMEM((block_count * shard_rows, lanes), jnp.float32),
            pltpu.VMEM((block_count, lanes), jnp.float32),
            pltpu.VMEM((shard_rows, lanes), jnp.float32),
            pltpu.SemaphoreType.DMA((3, CHUNKS)),
        ],
        compiler_params=limit(63),
        name="prepare",
    )(slots, gradient, second, after)


def released_kernel(*refs):
    pass


def released(arrays, other):
    count = len(arrays)
    return pl.pallas_call(
        released_kernel,
        out_shape=[jax.ShapeDtypeStruct(array.shape, array.dtype) for array in arrays],
        in_specs=[ANY] * (count + 1),
        out_specs=[ANY] * count,
        input_output_aliases={at: at for at in range(count)},
        compiler_params=limit(63),
        name="released",
    )(*arrays, other)


def together_kernel(columns, own, *refs):
    factors, out = refs[:PLACES], refs[PLACES]
    count, rows, part = columns.shape
    size = own.shape[0] * own.shape[1] // rows
    at_home = lax.div(place_here(), PLACES) == lax.axis_index("core")
    out[:count] = columns[...]
    for step in range(1, PLACES):
        out[count + step * size : count + (step + 1) * size] = factors[step][...].reshape(size, rows, part)

    @pl.when(at_home)
    def _():
        out[count : count + size] = own[...].reshape(size, rows, part)

    @pl.when(jnp.logical_not(at_home))
    def _():
        out[count : count + size] = factors[0][...].reshape(size, rows, part)


def together(columns, shards):
    count, rows, part = columns.shape
    count += PLACES * shards[0].shape[0] * shards[0].shape[1] // rows
    return pl.pallas_call(
        together_kernel,
        out_shape=jax.ShapeDtypeStruct((count, rows, part), columns.dtype),
        in_specs=[VMEM] * (1 + len(shards)),
        out_specs=VMEM,
        compiler_params=limit(16),
        name="together",
    )(columns, *shards)


def block_kernel(own, swapped, out, lf, rf, grad, half, full, notes):
    rows, part = own.shape[1:]
    order = lf.shape[0]
    count = COLS * RING
    groups = part // rows
    core = lax.axis_index("core")
    here = lax.axis_index("replica")
    place = lax.rem(place_here(), PLACES)

    @pl.when(place < SLOTS)
    def _():
        owner_core = lax.div(place_here(), PLACES)
        for b, held in enumerate((own, swapped)):
            h = core if b == 0 else 1 - core
            for col in range(COLS):
                for r in range(RING):
                    grad[col, h, :, r * part : (r + 1) * part] = held[member(col, r)]
            for step in range(PLACES):
                source = lax.rem(here + step + jnp.where(h == owner_core, 0, PLACES), RING)
                at = pl.ds(pl.multiple_of(source * part, part), part)
                for j in range(RING):
                    left = count + (2 * RING * step + j) * groups
                    right = left + RING * groups
                    lf[at, j * part : (j + 1) * part] = held[left : left + groups].reshape(part, part)
                    rf[j * part : (j + 1) * part, at] = held[right : right + groups].reshape(part, part)

        tile = 2 * part
        steps = order // tile

        def first(t, carry):
            at = pl.ds(pl.multiple_of(t * tile, tile), tile)
            rhs = grad[:, :, :, at].reshape(order, tile)
            half[:, at] = jnp.dot(lf[...], rhs, preferred_element_type=jnp.float32).astype(half.dtype)
            return carry

        lax.fori_loop(0, steps, first, 0, unroll=True)

        def second(t, square):
            at = pl.ds(pl.multiple_of(t * tile, tile), tile)
            value = jnp.dot(half[...], rf[:, at], preferred_element_type=jnp.float32)
            full[:, :, :, at] = value.reshape(COLS, CORES, rows, tile)
            return square + jnp.sum(value * value, axis=0, keepdims=True)

        square = lax.fori_loop(0, steps, second, jnp.zeros((1, tile), jnp.float32), unroll=True)
        square = jnp.sum(square, axis=1, keepdims=True)
        scale = 1.0 / jnp.sqrt(square + NORM_EPS)
        for r in range(RING):
            value = (full[:, core, :, r * part : (r + 1) * part] * scale).astype(out.dtype)
            for col in range(COLS):
                out[member(col, r)] = value[col]

    @pl.when(place == NOTE)
    def _():
        total = jnp.zeros(notes.shape, jnp.float32)
        for held in (own, swapped):
            total = total + jnp.sum(held[:count].astype(jnp.float32), axis=0)
        notes[...] = total
        for row in range(0, 2 * CORES * SLOTS, 2):
            high, low = high_low(notes[row : row + 1, :] + notes[row + 1 : row + 2, :])
            notes[row : row + 1, :] = high
            notes[row + 1 : row + 2, :] = low
        out[...] = jnp.broadcast_to(notes[...].astype(out.dtype), out.shape)


def precondition(own, swapped):
    _, rows, part = own.shape
    order = RING * part
    kind = own.dtype
    return pl.pallas_call(
        block_kernel,
        out_shape=jax.ShapeDtypeStruct((COLS * RING, rows, part), kind),
        in_specs=[VMEM] * 2,
        out_specs=VMEM,
        scratch_shapes=[
            pltpu.VMEM((order, order), kind),
            pltpu.VMEM((order, order), kind),
            pltpu.VMEM((COLS, CORES, rows, order), kind),
            pltpu.VMEM((order, order), kind),
            pltpu.VMEM((COLS, CORES, rows, order), jnp.float32),
            pltpu.VMEM((rows, part), jnp.float32),
        ],
        compiler_params=limit(28),
        cost_estimate=pl.CostEstimate(flops=4 * order**3, bytes_accessed=10 * order * order, transcendentals=0),
        name="precondition",
    )(own, swapped)


def finish_kernel(place, returned, momentum, out, wide, adam):
    block_rows, shard_rows, block_cols, lanes = momentum.shape
    for col in range(COLS):
        note = jnp.sum(returned[member(col, chip_of(NOTE))].astype(jnp.float32), axis=1, keepdims=True)
        adam[col * shard_rows : (col + 1) * shard_rows, :] = jnp.broadcast_to(note, (shard_rows, lanes))

    def step(i, carry):
        for j in range(block_cols):
            block = i * block_cols + j
            row = place[1, block]
            scale = jnp.sqrt(adam[pl.ds(row, 1), :] + adam[pl.ds(row + 1, 1), :])
            piece = returned[place[0, block]].astype(jnp.float32) * scale
            wide[pl.ds(j, shard_rows, stride=block_cols), :] = piece
        grafted = wide[...].reshape(shard_rows, block_cols, lanes)
        out[i] = (BETA_ONE * momentum[i].astype(jnp.float32) + grafted).astype(out.dtype)
        return carry

    lax.fori_loop(0, block_rows, step, 0, unroll=2)


def finish(place, returned, momentum):
    block_rows, shard_rows, block_cols, lanes = momentum.shape
    return pl.pallas_call(
        finish_kernel,
        out_shape=jax.ShapeDtypeStruct(momentum.shape, momentum.dtype),
        in_specs=[SMEM, VMEM, VMEM],
        out_specs=VMEM,
        scratch_shapes=[
            pltpu.VMEM((shard_rows * block_cols, lanes), jnp.float32),
            pltpu.VMEM((COLS * shard_rows, lanes), jnp.float32),
        ],
        compiler_params=limit(16),
        name="finish",
    )(place, returned, momentum)


def exchange(array):
    return lax.all_to_all(array, ("col", "replica"), split_axis=0, concat_axis=0, tiled=True)


def swap(array):
    return lax.ppermute(array, "core", [(0, 1), (1, 0)])


def local(gradient, second_moment, momentum, left_factor, right_factor, block_of_slot):
    spread = spread_factors(left_factor, right_factor)
    line = ("core", "replica")
    factors = [lax.ppermute(spread[step], line, factor_pairs(step)) for step in range(EARLY)]
    moment_new, pieces, place = prepare(block_of_slot.T, gradient, second_moment, spread[0])
    later = released(spread[EARLY:], pieces)
    factors += [lax.ppermute(shard, line, factor_pairs(EARLY + at)) for at, shard in enumerate(later)]
    columns = lax.cond(lax.axis_index("core") < CORES, exchange, jnp.zeros_like, pieces)
    held = together(columns, [spread[0]] + factors)
    parts = precondition(held, swap(held))
    return (finish(place, exchange(parts), momentum), moment_new)


def solution(mesh):
    fine = Mesh(mesh.devices.reshape(COLS, CORES, RING), ("col", "core", "replica"))
    fsdp = ("col", "core")
    in_specs = (
        P(None, fsdp, None, "replica"),
        P(None, fsdp, None, "replica"),
        P(None, fsdp, None, "replica"),
        P(fsdp, "replica", None),
        P(fsdp, None, "replica"),
        P(),
    )
    out_specs = (P(None, fsdp, None, "replica"), P(None, fsdp, None, "replica"))
    return jax.shard_map(local, mesh=fine, in_specs=in_specs, out_specs=out_specs, check_vma=False)
```
